32 devices in a mesh: dp: 8 (over y, x, core), blk: 4 (over z).
Axes of the slice: x: 2, y: 2, z: 4, core: 2. Of those that a mesh axis runs over, the one named last changes fastest.
Arguments:
- self_feat: bfloat16 [16384, 256], P(('dp', 'blk')), may hold values from -6 to 6
- nbr_mask: int32 [16384, 8], P(('dp', 'blk')), may hold values 0 or 1
- neighbour_slot: int32 [32, 4096], P(('dp', 'blk')), may hold values from 0 to 4095, each once within a row
- serve_rows: int32 [128, 1024], P(('dp', 'blk')), may hold values from 0 to 8191
- feat_store: bfloat16 [32768, 256], P('blk'), may hold values from -6 to 6
- w_self: bfloat16 [256, 1024], replicated, may hold values from -0.375 to 0.375
- w_nbr: bfloat16 [256, 1024], replicated, may hold values from -0.375 to 0.375
- w_out: bfloat16 [1024, 256], replicated, may hold values from -0.1875 to 0.1875
Outputs:
- grad_self: float32 [256, 1024], replicated
- grad_nbr: float32 [256, 1024], replicated
- grad_out: float32 [1024, 256], replicated
The draws below stay inside these ranges and needn't reach their ends.
All inputs are finite; a program needn't handle non-finite values. No bound on the sum of `nbr_mask` on one device may be relied on, other than what follows from the above.
Results may differ from the reference program's by a relative error of at most 0.0077.
Values may be sent and summed in bfloat16 or wider, within the bound.
No kernel may reach another device: no remote copies, remote signals or barrier semaphores. Data moves between devices by JAX's collectives and lax.ppermute only.
A program may use at most 64 MiB of HBM per device.

```python
import jax
import jax.numpy as jnp
from jax import lax

INPUT_WIDTH = 256
HID = 1024
D_OUT = 256
PAIRS_DEV = 256
FANOUT = 8
STORE_DEV = 8192
NEIGHBOUR_SLOTS = 4096
CAP = 1024
NODES = 16384
N_DP = 8
N_BLK = 4


def set_ends(array, own_key, smallest, top_value):
    index_at = [jax.random.randint(jax.random.fold_in(own_key, axis), (), 0, length) for axis, length in enumerate(array.shape)]
    main_axis = array.shape.index(max(array.shape))
    neighbour = index_at[:main_axis] + [(index_at[main_axis] + 1) % array.shape[main_axis]] + index_at[main_axis + 1:]
    return array.at[tuple(index_at)].set(smallest).at[tuple(neighbour)].set(top_value)


def block_levels(own_key, extent, cuts, low, high):
    def one(axis_at, shards_of):
        draws = jax.random.uniform(jax.random.fold_in(jax.random.fold_in(own_key, 6), axis_at), (shards_of,), jnp.float32, low / len(cuts), high / len(cuts))
        return jnp.repeat(jnp.exp(draws), extent[axis_at] // shards_of).reshape((-1,) + (1,) * (len(extent) - axis_at - 1))

    level = one(*cuts[0])
    for cut in cuts[1:]:
        level = level * one(*cut)
    return level


def scatter_about(own_key, extent, width, reach, shards=(), kind=jnp.bfloat16):
    factor_of = block_levels(own_key, extent, shards, -0.22, 0.18) if shards else 1.0
    array = jax.random.normal(own_key, extent, jnp.float32) * width * factor_of
    return jnp.minimum(jnp.maximum(array, -reach), reach).astype(kind)


def setup_inputs(seed: int = 0) -> dict:
    key_list = jax.random.split(jax.random.key(seed), 9)
    self_feat = scatter_about(key_list[0], (NODES, INPUT_WIDTH), 1.0, 6.0, ((0, 32),))
    nbr_mask = set_ends((jax.random.randint(key_list[1], (NODES, FANOUT), 0, 4) < 3).astype(jnp.int32), jax.random.fold_in(key_list[1], 1), 0, 1)
    neighbour_slot = jax.vmap(lambda own: jax.random.permutation(own, NEIGHBOUR_SLOTS))(jax.random.split(key_list[2], (N_DP * N_BLK))).reshape((N_DP * N_BLK, NEIGHBOUR_SLOTS)).astype(jnp.int32)
    serve_rows = set_ends(jax.random.randint(key_list[3], (N_DP * N_BLK * N_BLK, CAP), 0, STORE_DEV), jax.random.fold_in(key_list[3], 1), 0, STORE_DEV - 1).astype(jnp.int32)
    feat_store = scatter_about(key_list[4], (N_BLK * STORE_DEV, INPUT_WIDTH), 1.0, 6.0, ((0, 4),))
    w_self = scatter_about(key_list[5], (INPUT_WIDTH, HID), INPUT_WIDTH ** -0.5, 0.375)
    w_nbr = scatter_about(key_list[6], (INPUT_WIDTH, HID), INPUT_WIDTH ** -0.5, 0.375)
    w_out = scatter_about(key_list[7], (HID, D_OUT), HID ** -0.5, 0.1875)
    return {"self_feat": self_feat, "nbr_mask": nbr_mask, "neighbour_slot": neighbour_slot, "serve_rows": serve_rows, "feat_store": feat_store, "w_self": w_self, "w_nbr": w_nbr, "w_out": w_out}


MARGIN = 0.5

def forward_nodes(self_rows, node_mask, neighbours, w_self, w_nbr, w_out):
    first_col = lax.broadcasted_iota(jnp.int32, node_mask.shape, 1) == 0
    valid_slots = jnp.where(first_col, 1, node_mask).astype(jnp.float32)
    live_count = lax.optimization_barrier(jnp.sum(valid_slots, 1, keepdims=True))
    pooled = (lax.optimization_barrier(jnp.sum(neighbours.astype(jnp.float32) * valid_slots[:, :, None], 1)) / live_count).astype(jnp.bfloat16)
    pre_act = jnp.dot(self_rows, w_self, preferred_element_type=jnp.float32) + jnp.dot(pooled, w_nbr, preferred_element_type=jnp.float32)
    hidden = (pre_act * jax.nn.sigmoid(pre_act)).astype(jnp.bfloat16)
    projected = jnp.dot(hidden, w_out, preferred_element_type=jnp.float32)
    inv_norm = lax.rsqrt(lax.optimization_barrier(jnp.mean(projected * projected, 1, keepdims=True)) + 1e-06)
    embedding = (projected * inv_norm).astype(jnp.bfloat16)
    return (pooled, pre_act, hidden, projected, inv_norm, embedding)

def pair_weights(queries, own_items, cycle_items, position):
    score_scale = queries.shape[1] ** (-0.5)
    scores = jnp.dot(queries, cycle_items.T, preferred_element_type=jnp.float32) * score_scale
    positive_item = lax.optimization_barrier(jnp.sum(queries.astype(jnp.float32) * own_items.astype(jnp.float32), 1, keepdims=True)) * score_scale
    weights = jax.nn.sigmoid(scores - positive_item + MARGIN) / scores.shape[1]
    columns = lax.broadcasted_iota(jnp.int32, scores.shape, 1)
    own_column = lax.broadcasted_iota(jnp.int32, scores.shape, 0) + position * queries.shape[0]
    row_total = lax.optimization_barrier(jnp.sum(weights, 1, keepdims=True))
    return jnp.where(columns == own_column, weights - row_total, weights).astype(jnp.bfloat16)

def backward_nodes(self_rows, pooled, pre_act, hidden, projected, inv_norm, d_embed, w_out):
    contract = (((0,), (0,)), ((), ()))
    interior_term = lax.optimization_barrier(jnp.mean(d_embed * projected, 1, keepdims=True))
    d_proj = (inv_norm * d_embed - projected * inv_norm ** 3 * interior_term).astype(jnp.bfloat16)
    g_out = lax.dot_general(hidden, d_proj, contract, preferred_element_type=jnp.float32)
    d_hidden = lax.dot_general(d_proj, w_out, (((1,), (1,)), ((), ())), preferred_element_type=jnp.float32)
    gate_sig = jax.nn.sigmoid(pre_act)
    d_pre = (d_hidden * gate_sig * (1.0 + pre_act * (1.0 - gate_sig))).astype(jnp.bfloat16)
    g_self = lax.dot_general(self_rows, d_pre, contract, preferred_element_type=jnp.float32)
    g_nbr = lax.dot_general(pooled, d_pre, contract, preferred_element_type=jnp.float32)
    return (g_self, g_nbr, g_out)

def reference(self_feat, nbr_mask, neighbour_slot, serve_rows, feat_store, w_self, w_nbr, w_out):
    table = feat_store.reshape(N_BLK, STORE_DEV, INPUT_WIDTH)
    feats = self_feat.reshape(N_DP, N_BLK, 2 * PAIRS_DEV, INPUT_WIDTH)
    masks = nbr_mask.reshape(N_DP, N_BLK, 2 * PAIRS_DEV, FANOUT)
    slot_entries = neighbour_slot.reshape(N_DP, N_BLK, NEIGHBOUR_SLOTS)
    serves = serve_rows.reshape(N_DP, N_BLK, N_BLK, CAP)
    score_scale = D_OUT ** (-0.5)
    positions = jnp.arange(N_BLK, dtype=jnp.int32)

    def one_group(carry, packed):
        feat_group, mask_group, slot_group, serve_group = packed
        dispatched_rows = jax.vmap(lambda part_table, index_list: part_table[index_list])(table, serve_group)
        received_rows = jnp.swapaxes(dispatched_rows, 0, 1).reshape(N_BLK, NEIGHBOUR_SLOTS, INPUT_WIDTH)
        neighbours = jax.vmap(lambda got_rows, order: got_rows[order])(received_rows, slot_group)
        neighbours = neighbours.reshape(N_BLK, 2 * PAIRS_DEV, FANOUT, INPUT_WIDTH)
        saved = jax.vmap(forward_nodes, in_axes=(0, 0, 0, None, None, None))(feat_group, mask_group, neighbours, w_self, w_nbr, w_out)
        pooled, pre_act, hidden, projected, inv_norm, embedding = saved
        queries = embedding[:, :PAIRS_DEV]
        own_items = embedding[:, PAIRS_DEV:]
        cycle_items = own_items.reshape(N_BLK * PAIRS_DEV, D_OUT)
        weight_tile = jax.vmap(pair_weights, in_axes=(0, 0, None, 0))(queries, own_items, cycle_items, positions)
        d_query = jax.vmap(lambda tile: jnp.dot(tile, cycle_items, preferred_element_type=jnp.float32))(weight_tile) * score_scale
        d_items = jnp.einsum('bpj,bpd->jd', weight_tile.astype(jnp.float32), queries.astype(jnp.float32)) * score_scale
        d_embed = jnp.concatenate([d_query, d_items.reshape(N_BLK, PAIRS_DEV, D_OUT)], 1)
        grads = jax.vmap(backward_nodes, in_axes=(0, 0, 0, 0, 0, 0, 0, None))(feat_group, pooled, pre_act, hidden, projected, inv_norm, d_embed, w_out)
        return (tuple((total + lax.optimization_barrier(jnp.sum(part_grad, 0)) for total, part_grad in zip(carry, grads))), None)
    start = (jnp.zeros((INPUT_WIDTH, HID), jnp.float32), jnp.zeros((INPUT_WIDTH, HID), jnp.float32), jnp.zeros((HID, D_OUT), jnp.float32))
    totals, _ = lax.scan(one_group, start, (feats, masks, slot_entries, serves))
    return (totals[0], totals[1], totals[2])
```

```python
import jax
import jax.numpy as jnp
from jax import lax
from jax.sharding import PartitionSpec as P

MARGIN = 0.5
AXES = ("dp", "blk")
BF16 = jnp.bfloat16
F32 = jnp.float32
OVER_ROWS = (((0,), (0,)), ((), ()))


def exchange(value, sizes, flip_dp, flip_blk):
    dp_size, blk_size = sizes
    pairs = [
        (g * blk_size + b, (g ^ flip_dp) * blk_size + (b ^ flip_blk))
        for g in range(dp_size)
        for b in range(blk_size)
    ]
    return lax.ppermute(value, AXES, pairs)


def block_of(array, index, count):
    rows = array.shape[0] // count
    return lax.dynamic_slice_in_dim(array, index * rows, rows, 0)


def in_order(parts, own):
    ordered = []
    for place in range(len(parts)):
        block = parts[place]
        for own_value in range(1, len(parts)):
            block = jnp.where(own == own_value, parts[place ^ own_value], block)
        ordered.append(block)
    return jnp.concatenate(ordered, 0)


def reduce_blocks(array, own, count, send):
    arrived = [send(block_of(array, own ^ j, count).astype(BF16), j) for j in range(1, count)]
    total = block_of(array, own, count)
    for part in arrived:
        total = total + part.astype(F32)
    return total


def gather_blocks(block, own, count, send):
    return in_order([block] + [send(block, j) for j in range(1, count)], own)


def node_of_arrival(neighbour_slot, valid, count):
    slots = neighbour_slot.shape[1]
    low = 128
    node = lax.broadcasted_iota(jnp.int32, (1, slots), 1) // (slots // valid.shape[0])
    flat_valid = valid.reshape(1, slots)
    high_hot = lax.broadcasted_iota(jnp.int32, (slots // low, slots), 0) == neighbour_slot // low
    low_hot = lax.broadcasted_iota(jnp.int32, (low, slots), 0) == neighbour_slot % low
    upper = ((node // 16 + 1) * flat_valid).astype(F32)
    lower = ((node % 16) * flat_valid).astype(F32)
    codes = jnp.concatenate(
        [jnp.where(low_hot, upper, 0.0), jnp.where(low_hot, lower, 0.0)], 0
    ).astype(BF16)
    found = lax.dot_general(
        high_hot.astype(BF16), codes, (((1,), (1,)), ((), ())), preferred_element_type=F32
    )
    found = found.astype(jnp.int32)
    return ((found[:, :low] - 1) * 16 + found[:, low:]).reshape(count, slots // count)


def pooled_mean(nbr_mask, neighbour_slot, serve_rows, feat_store, own, sizes):
    blk_size = sizes[1]
    nodes = nbr_mask.shape[0]
    first_col = lax.broadcasted_iota(jnp.int32, nbr_mask.shape, 1) == 0
    valid = jnp.where(first_col, 1, nbr_mask)
    live_count = jnp.sum(valid.astype(F32), 1, keepdims=True)
    node_at = node_of_arrival(neighbour_slot, valid, blk_size)
    order = sorted(range(1, blk_size), key=lambda j: (j != blk_size // 2, j))
    wanted = {
        j: exchange(block_of(node_at, own ^ j, blk_size), sizes, 0, j) for j in order
    }
    wanted[0] = block_of(node_at, own, blk_size)
    row_node = lax.broadcasted_iota(jnp.int32, (nodes, serve_rows.shape[1]), 0)
    total = None
    for j in order + [0]:
        served = block_of(serve_rows, own ^ j, blk_size)[0]
        rows = feat_store.at[served].get(mode="promise_in_bounds")
        pick = (row_node == wanted[j]).astype(BF16)
        part = jnp.dot(pick, rows, preferred_element_type=F32)
        if j:
            part = exchange(part.astype(BF16), sizes, 0, j).astype(F32)
        total = part if total is None else total + part
    return (total / live_count).astype(BF16)


def pair_gradients(embedding, own, sizes):
    blk_size = sizes[1]
    pairs = embedding.shape[0] // 2
    scale = embedding.shape[1] ** (-0.5)
    queries, items = embedding[:pairs], embedding[pairs:]
    order = sorted(range(1, blk_size), key=lambda j: (j != blk_size // 2, j))
    other_items = [exchange(items, sizes, 0, j) for j in order]
    other_queries = [exchange(queries, sizes, 0, j) for j in order]
    cycle = jnp.concatenate([items] + other_items, 0)
    columns = cycle.shape[0]

    def positive_of(q, i):
        return jnp.sum(q.astype(F32) * i.astype(F32), 1, keepdims=True) * scale

    def weights_of(q, i, positive):
        scores = lax.dot_general(q, i, (((1,), (1,)), ((), ())), preferred_element_type=F32)
        return jax.nn.sigmoid(scores * scale - positive + MARGIN) / columns

    weights = weights_of(queries, cycle, positive_of(queries, items))
    row_total = jnp.sum(weights, 1, keepdims=True)
    diagonal = lax.broadcasted_iota(jnp.int32, weights.shape, 0) == lax.broadcasted_iota(
        jnp.int32, weights.shape, 1
    )
    tile = jnp.where(diagonal, weights - row_total, weights).astype(BF16)
    d_query = jnp.dot(tile, cycle, preferred_element_type=F32) * scale
    remote_queries = jnp.concatenate(other_queries, 0)
    remote_tile = weights_of(
        remote_queries, items, positive_of(remote_queries, cycle[pairs:])
    ).astype(BF16)
    d_item = (
        lax.dot_general(tile[:, :pairs], queries, OVER_ROWS, preferred_element_type=F32)
        + lax.dot_general(remote_tile, remote_queries, OVER_ROWS, preferred_element_type=F32)
    ) * scale
    return jnp.concatenate([d_query, d_item], 0)


def sum_staged(g_in, g_out, group, own, sizes):
    dp_size, blk_size = sizes
    width = g_in.shape[1]
    side = g_out.shape[1]
    plane = dp_size // 2
    core = group % 2
    across = group // 2

    def half(index):
        g_in_half = block_of(g_in, index, 2)
        g_out_half = block_of(g_out, index, 2)
        rows = g_out_half.shape[0] * side // width
        folded = jnp.concatenate(
            [g_out_half[k * rows : (k + 1) * rows] for k in range(width // side)], 1
        )
        return jnp.concatenate([g_in_half, folded], 0)

    def unfold(folded):
        return jnp.concatenate(
            [folded[:, k * side : (k + 1) * side] for k in range(width // side)], 0
        )

    def over_core(v, j):
        return exchange(v, sizes, j, 0)

    def over_plane(v, j):
        return exchange(v, sizes, 2 * j, 0)

    def over_blk(v, j):
        return exchange(v, sizes, 0, j)

    total = half(core) + over_core(half(1 - core).astype(BF16), 1).astype(F32)
    total = reduce_blocks(total, across, plane, over_plane)
    total = reduce_blocks(total, own, blk_size, over_blk)
    block = total.astype(BF16)
    block = gather_blocks(block, own, blk_size, over_blk)
    block = gather_blocks(block, across, plane, over_plane)
    other = over_core(block, 1)
    first = jnp.where(core == 0, block, other)
    second = jnp.where(core == 0, other, block)
    cut = g_in.shape[0] // 2
    grad_out = jnp.concatenate([unfold(first[cut:]), unfold(second[cut:])], 0)
    return (first[:cut].astype(F32), second[:cut].astype(F32), grad_out.astype(F32))


def on_device(sizes, self_feat, nbr_mask, neighbour_slot, serve_rows, feat_store, w_self, w_nbr, w_out):
    dp_size, blk_size = sizes
    group = lax.axis_index("dp")
    own = lax.axis_index("blk")
    pooled = pooled_mean(nbr_mask, neighbour_slot, serve_rows, feat_store, own, sizes)
    pre_act = jnp.dot(self_feat, w_self, preferred_element_type=F32) + jnp.dot(
        pooled, w_nbr, preferred_element_type=F32
    )
    gate_sig = jax.nn.sigmoid(pre_act)
    hidden = (pre_act * gate_sig).astype(BF16)
    projected = jnp.dot(hidden, w_out, preferred_element_type=F32)
    inv_norm = lax.rsqrt(jnp.mean(projected * projected, 1, keepdims=True) + 1e-06)
    embedding = (projected * inv_norm).astype(BF16)
    d_embed = pair_gradients(embedding, own, sizes)
    interior_term = jnp.mean(d_embed * projected, 1, keepdims=True)
    d_proj = (inv_norm * d_embed - projected * inv_norm**3 * interior_term).astype(BF16)
    g_out = lax.dot_general(hidden, d_proj, OVER_ROWS, preferred_element_type=F32)
    d_hidden = lax.dot_general(d_proj, w_out, (((1,), (1,)), ((), ())), preferred_element_type=F32)
    d_pre = (d_hidden * gate_sig * (1.0 + pre_act * (1.0 - gate_sig))).astype(BF16)
    inputs = jnp.concatenate([self_feat, pooled], 1)
    g_in = lax.dot_general(inputs, d_pre, OVER_ROWS, preferred_element_type=F32)
    staged = (dp_size & (dp_size - 1)) == 0 and dp_size > 1
    if staged and g_in.shape[0] % (8 * dp_size * blk_size) == 0:
        return sum_staged(g_in, g_out, group, own, sizes)
    g_in, grad_out = lax.psum((g_in, g_out), AXES)
    cut = g_in.shape[0] // 2
    return (g_in[:cut], g_in[cut:], grad_out)


def solution(mesh):
    sizes = (mesh.shape["dp"], mesh.shape["blk"])
    in_specs = (
        P(("dp", "blk"), None),
        P(("dp", "blk"), None),
        P(("dp", "blk"), None),
        P(("dp", "blk"), None),
        P("blk", None),
        P(),
        P(),
        P(),
    )
    out_specs = (P(), P(), P())

    def body(*arrays):
        return on_device(sizes, *arrays)

    return jax.shard_map(
        body, mesh=mesh, in_specs=in_specs, out_specs=out_specs, check_vma=False
    )
```

```python
import jax
import jax.numpy as jnp
from jax import lax
from jax.sharding import PartitionSpec as P

MARGIN = 0.5
AXES = ("dp", "blk")
BF16 = jnp.bfloat16
F32 = jnp.float32
OVER_ROWS = (((0,), (0,)), ((), ()))


def exchange(value, sizes, flip_dp, flip_blk):
    dp_size, blk_size = sizes
    pairs = [
        (g * blk_size + b, (g ^ flip_dp) * blk_size + (b ^ flip_blk))
        for g in range(dp_size)
        for b in range(blk_size)
    ]
    return lax.ppermute(value, AXES, pairs)


def block_of(array, index, count):
    rows = array.shape[0] // count
    return lax.dynamic_slice_in_dim(array, index * rows, rows, 0)


def in_order(parts, own):
    ordered = []
    for place in range(len(parts)):
        block = parts[place]
        for own_value in range(1, len(parts)):
            block = jnp.where(own == own_value, parts[place ^ own_value], block)
        ordered.append(block)
    return jnp.concatenate(ordered, 0)


def reduce_blocks(array, own, count, send):
    arrived = [send(block_of(array, own ^ j, count).astype(BF16), j) for j in range(1, count)]
    total = block_of(array, own, count)
    for part in arrived:
        total = total + part.astype(F32)
    return total


def gather_blocks(block, own, count, send):
    return in_order([block] + [send(block, j) for j in range(1, count)], own)


def node_of_arrival(neighbour_slot, valid, count):
    slots = neighbour_slot.shape[1]
    low = 128
    node = lax.broadcasted_iota(jnp.int32, (1, slots), 1) // (slots // valid.shape[0])
    flat_valid = valid.reshape(1, slots)
    high_hot = lax.broadcasted_iota(jnp.int32, (slots // low, slots), 0) == neighbour_slot // low
    low_hot = lax.broadcasted_iota(jnp.int32, (low, slots), 0) == neighbour_slot % low
    upper = ((node // 16 + 1) * flat_valid).astype(F32)
    lower = ((node % 16) * flat_valid).astype(F32)
    codes = jnp.concatenate(
        [jnp.where(low_hot, upper, 0.0), jnp.where(low_hot, lower, 0.0)], 0
    ).astype(BF16)
    found = lax.dot_general(
        high_hot.astype(BF16), codes, (((1,), (1,)), ((), ())), preferred_element_type=F32
    )
    found = found.astype(jnp.int32)
    return ((found[:, :low] - 1) * 16 + found[:, low:]).reshape(count, slots // count)


def pooled_mean(nbr_mask, neighbour_slot, serve_rows, feat_store, own, sizes):
    blk_size = sizes[1]
    nodes = nbr_mask.shape[0]
    first_col = lax.broadcasted_iota(jnp.int32, nbr_mask.shape, 1) == 0
    valid = jnp.where(first_col, 1, nbr_mask)
    live_count = jnp.sum(valid.astype(F32), 1, keepdims=True)
    node_at = node_of_arrival(neighbour_slot, valid, blk_size)
    order = sorted(range(1, blk_size), key=lambda j: (j < blk_size // 2, j))
    wanted = {
        j: exchange(block_of(node_at, own ^ j, blk_size), sizes, 0, j) for j in order
    }
    wanted[0] = block_of(node_at, own, blk_size)
    row_node = lax.broadcasted_iota(jnp.int32, (nodes, serve_rows.shape[1]), 0)
    total = None
    sent = None
    for j in order + [0]:
        served = block_of(serve_rows, own ^ j, blk_size)[0]
        if sent is not None:
            served, sent = lax.optimization_barrier((served, sent))
            arrived = exchange(sent, sizes, 0, previous).astype(F32)
            total = arrived if total is None else total + arrived
        rows = feat_store.at[served].get(mode="promise_in_bounds")
        pick = (row_node == wanted[j]).astype(BF16)
        part = jnp.dot(pick, rows, preferred_element_type=F32)
        sent, previous = part.astype(BF16), j
    return ((total + part) / live_count).astype(BF16)


def spread(block, sizes):
    blk_size = sizes[1]
    known = {0: block}
    bit = blk_size // 2
    while bit:
        known.update({j ^ bit: exchange(v, sizes, 0, bit) for j, v in list(known.items())})
        bit //= 2
    return [known[j] for j in range(1, blk_size)]


def pair_gradients(queries, items, sizes):
    pairs = queries.shape[0]
    scale = queries.shape[1] ** (-0.5)
    other_items = spread(items, sizes)
    other_queries = spread(queries, sizes)
    cycle = jnp.concatenate([items] + other_items, 0)
    columns = cycle.shape[0]

    def positive_of(q, i):
        return jnp.sum(q.astype(F32) * i.astype(F32), 1, keepdims=True) * scale

    def weights_of(q, i, positive):
        scores = lax.dot_general(q, i, (((1,), (1,)), ((), ())), preferred_element_type=F32)
        return jax.nn.sigmoid(scores * scale - positive + MARGIN) / columns

    weights = weights_of(queries, cycle, positive_of(queries, items))
    row_total = jnp.sum(weights, 1, keepdims=True)
    tile = weights.astype(BF16)
    d_query = (
        jnp.dot(tile, cycle, preferred_element_type=F32) - row_total * items.astype(F32)
    ) * scale
    remote_queries = jnp.concatenate(other_queries, 0)
    remote_tile = weights_of(
        remote_queries, items, positive_of(remote_queries, cycle[pairs:])
    ).astype(BF16)
    d_item = (
        lax.dot_general(tile[:, :pairs], queries, OVER_ROWS, preferred_element_type=F32)
        + lax.dot_general(remote_tile, remote_queries, OVER_ROWS, preferred_element_type=F32)
        - row_total * queries.astype(F32)
    ) * scale
    return d_query, d_item


def sum_staged(g_in, g_out, group, own, sizes):
    dp_size, blk_size = sizes
    width = g_in.shape[1]
    side = g_out.shape[1]
    plane = dp_size // 2
    core = group % 2
    across = group // 2

    def half(index):
        g_in_half = block_of(g_in, index, 2)
        g_out_half = block_of(g_out, index, 2)
        rows = g_out_half.shape[0] * side // width
        folded = jnp.concatenate(
            [g_out_half[k * rows : (k + 1) * rows] for k in range(width // side)], 1
        )
        return jnp.concatenate([g_in_half, folded], 0)

    def unfold(folded):
        return jnp.concatenate(
            [folded[:, k * side : (k + 1) * side] for k in range(width // side)], 0
        )

    def over_core(v, j):
        return exchange(v, sizes, j, 0)

    def over_plane(v, j):
        return exchange(v, sizes, 2 * j, 0)

    def over_blk(v, j):
        return exchange(v, sizes, 0, j)

    total = half(core) + over_core(half(1 - core).astype(BF16), 1).astype(F32)
    total = reduce_blocks(total, across, plane, over_plane)
    total = reduce_blocks(total, own, blk_size, over_blk)
    block = total.astype(BF16)
    block = gather_blocks(block, own, blk_size, over_blk)
    block = gather_blocks(block, across, plane, over_plane)
    other = over_core(block, 1)
    first = jnp.where(core == 0, block, other)
    second = jnp.where(core == 0, other, block)
    cut = g_in.shape[0] // 2
    grad_out = jnp.concatenate([unfold(first[cut:]), unfold(second[cut:])], 0)
    return (first[:cut].astype(F32), second[:cut].astype(F32), grad_out.astype(F32))


def on_device(sizes, self_feat, nbr_mask, neighbour_slot, serve_rows, feat_store, w_self, w_nbr, w_out):
    dp_size, blk_size = sizes
    group = lax.axis_index("dp")
    own = lax.axis_index("blk")
    pooled = pooled_mean(nbr_mask, neighbour_slot, serve_rows, feat_store, own, sizes)
    pre_act = jnp.dot(self_feat, w_self, preferred_element_type=F32) + jnp.dot(
        pooled, w_nbr, preferred_element_type=F32
    )
    gate_sig = jax.nn.sigmoid(pre_act)
    hidden = (pre_act * gate_sig).astype(BF16)
    projected = jnp.dot(hidden, w_out, preferred_element_type=F32)
    inv_norm = lax.rsqrt(jnp.mean(projected * projected, 1, keepdims=True) + 1e-06)
    embedding = (projected * inv_norm).astype(BF16)
    pairs = embedding.shape[0] // 2
    inputs = jnp.concatenate([self_feat, pooled], 1)
    g_in = g_out = 0.0
    for half, d_embed in enumerate(pair_gradients(embedding[:pairs], embedding[pairs:], sizes)):
        rows = slice(half * pairs, (half + 1) * pairs)
        inv, proj, pre, sig = inv_norm[rows], projected[rows], pre_act[rows], gate_sig[rows]
        interior_term = jnp.mean(d_embed * proj, 1, keepdims=True)
        d_proj = (inv * d_embed - proj * inv**3 * interior_term).astype(BF16)
        d_hidden = lax.dot_general(
            d_proj, w_out, (((1,), (1,)), ((), ())), preferred_element_type=F32
        )
        d_pre = (d_hidden * sig * (1.0 + pre * (1.0 - sig))).astype(BF16)
        g_out += lax.dot_general(hidden[rows], d_proj, OVER_ROWS, preferred_element_type=F32)
        g_in += lax.dot_general(inputs[rows], d_pre, OVER_ROWS, preferred_element_type=F32)
    staged = (dp_size & (dp_size - 1)) == 0 and dp_size > 1
    if staged and g_in.shape[0] % (8 * dp_size * blk_size) == 0:
        return sum_staged(g_in, g_out, group, own, sizes)
    g_in, grad_out = lax.psum((g_in, g_out), AXES)
    cut = g_in.shape[0] // 2
    return (g_in[:cut], g_in[cut:], grad_out)


def solution(mesh):
    sizes = (mesh.shape["dp"], mesh.shape["blk"])
    in_specs = (
        P(("dp", "blk"), None),
        P(("dp", "blk"), None),
        P(("dp", "blk"), None),
        P(("dp", "blk"), None),
        P("blk", None),
        P(),
        P(),
        P(),
    )
    out_specs = (P(), P(), P())

    def body(*arrays):
        return on_device(sizes, *arrays)

    return jax.shard_map(
        body, mesh=mesh, in_specs=in_specs, out_specs=out_specs, check_vma=False
    )
```

```python
import functools

import jax
import jax.numpy as jnp
from jax import lax
from jax.experimental import pallas as pl
from jax.experimental.pallas import tpu as pltpu
from jax.sharding import PartitionSpec as P

MARGIN = 0.5
AXES = ("dp", "blk")
BF16 = jnp.bfloat16
F32 = jnp.float32
OVER_ROWS = (((0,), (0,)), ((), ()))
LAST_DIMS = (((1,), (1,)), ((), ()))


def exchange(value, sizes, flip_dp, flip_blk):
    dp_size, blk_size = sizes
    pairs = [
        (g * blk_size + b, (g ^ flip_dp) * blk_size + (b ^ flip_blk))
        for g in range(dp_size)
        for b in range(blk_size)
    ]
    return lax.ppermute(value, AXES, pairs)


def block_of(array, index, count):
    rows = array.shape[0] // count
    return lax.dynamic_slice_in_dim(array, index * rows, rows, 0)


def in_order(parts, own):
    ordered = []
    for place in range(len(parts)):
        block = parts[place]
        for own_value in range(1, len(parts)):
            block = jnp.where(own == own_value, parts[place ^ own_value], block)
        ordered.append(block)
    return jnp.concatenate(ordered, 0)


def reduce_blocks(array, own, count, send):
    arrived = [send(block_of(array, own ^ j, count).astype(BF16), j) for j in range(1, count)]
    total = block_of(array, own, count)
    for part in arrived:
        total = total + part.astype(F32)
    return total


def gather_blocks(block, own, count, send):
    return in_order([block] + [send(block, j) for j in range(1, count)], own)


def node_of_arrival(neighbour_slot, valid, count):
    slots = neighbour_slot.shape[1]
    low = 128
    node = lax.broadcasted_iota(jnp.int32, (1, slots), 1) // (slots // valid.shape[0])
    flat_valid = valid.reshape(1, slots)
    high_hot = lax.broadcasted_iota(jnp.int32, (slots // low, slots), 0) == neighbour_slot // low
    low_hot = lax.broadcasted_iota(jnp.int32, (low, slots), 0) == neighbour_slot % low
    upper = ((node // 16 + 1) * flat_valid).astype(F32)
    lower = ((node % 16) * flat_valid).astype(F32)
    codes = jnp.concatenate(
        [jnp.where(low_hot, upper, 0.0), jnp.where(low_hot, lower, 0.0)], 0
    ).astype(BF16)
    found = lax.dot_general(
        high_hot.astype(BF16), codes, (((1,), (1,)), ((), ())), preferred_element_type=F32
    )
    found = found.astype(jnp.int32)
    return ((found[:, :low] - 1) * 16 + found[:, low:]).reshape(count, slots // count)


def pooled_mean(nbr_mask, neighbour_slot, serve_rows, feat_store, own, sizes):
    blk_size = sizes[1]
    nodes = nbr_mask.shape[0]
    first_col = lax.broadcasted_iota(jnp.int32, nbr_mask.shape, 1) == 0
    valid = jnp.where(first_col, 1, nbr_mask)
    live_count = jnp.sum(valid.astype(F32), 1, keepdims=True)
    node_at = node_of_arrival(neighbour_slot, valid, blk_size)
    order = sorted(range(1, blk_size), key=lambda j: (j < blk_size // 2, j))
    wanted = {
        j: exchange(block_of(node_at, own ^ j, blk_size), sizes, 0, j) for j in order
    }
    wanted[0] = block_of(node_at, own, blk_size)
    row_node = lax.broadcasted_iota(jnp.int32, (nodes, serve_rows.shape[1]), 0)
    total = None
    sent = None
    for j in order + [0]:
        served = block_of(serve_rows, own ^ j, blk_size)[0]
        if sent is not None:
            served, sent = lax.optimization_barrier((served, sent))
            arrived = exchange(sent, sizes, 0, previous).astype(F32)
            total = arrived if total is None else total + arrived
        rows = feat_store.at[served].get(mode="promise_in_bounds")
        pick = (row_node == wanted[j]).astype(BF16)
        part = jnp.dot(pick, rows, preferred_element_type=F32)
        sent, previous = part.astype(BF16), j
    return ((total + part) / live_count).astype(BF16)


def spread(block, sizes):
    blk_size = sizes[1]
    known = {0: block}
    bit = blk_size // 2
    while bit:
        known.update({j ^ bit: exchange(v, sizes, 0, bit) for j, v in list(known.items())})
        bit //= 2
    return [known[j] for j in range(1, blk_size)]


def pair_weights(q, i, positive, scale, columns):
    scores = lax.dot_general(q, i, LAST_DIMS, preferred_element_type=F32)
    return jax.nn.sigmoid(scores * scale - positive + MARGIN) / columns


def positive_of(q, i, scale):
    return jnp.sum(q.astype(F32) * i.astype(F32), 1, keepdims=True) * scale


def through_norm(d_embed, proj, inv):
    interior = jnp.mean(d_embed * proj, 1, keepdims=True)
    return (inv * d_embed - proj * inv**3 * interior).astype(BF16)


def through_gate(d_proj, pre, w_out):
    d_hidden = lax.dot_general(d_proj, w_out, LAST_DIMS, preferred_element_type=F32)
    sig = jax.nn.sigmoid(pre)
    return (d_hidden * sig * (1.0 + pre * (1.0 - sig))).astype(BF16)


def query_kernel(group_size, *refs):
    queries, items = refs[0], refs[1 : 1 + group_size]
    proj, inv, pre, w_out, tile, row_total, d_proj, d_pre = refs[1 + group_size :]
    q, own_items = queries[...], items[0][...]
    pairs, width = q.shape
    scale = width ** (-0.5)
    positive = positive_of(q, own_items, scale)
    total = jnp.zeros((pairs, 1), F32)
    d_query = jnp.zeros((pairs, width), F32)
    for j in range(group_size):
        block = items[j][...]
        weights = pair_weights(q, block, positive, scale, group_size * pairs)
        total += jnp.sum(weights, 1, keepdims=True)
        rounded = weights.astype(BF16)
        if j == 0:
            tile[...] = rounded
        d_query += jnp.dot(rounded, block, preferred_element_type=F32)
    row_total[...] = total
    d_query = (d_query - total * own_items.astype(F32)) * scale
    d_p = through_norm(d_query, proj[:pairs], inv[:pairs])
    d_proj[...] = d_p
    d_pre[...] = through_gate(d_p, pre[:pairs], w_out[...])


def item_kernel(group_size, core_ref, *refs):
    queries, items = refs[:group_size], refs[group_size : 2 * group_size]
    (tile, row_total, proj, inv, pre, w_out, d_proj_q, d_pre_q, hidden, inputs, keep, give) = refs[
        2 * group_size :
    ]
    own_items, q = items[0][...], queries[0][...]
    pairs, width = q.shape
    scale = width ** (-0.5)
    d_item = (
        lax.dot_general(tile[...], q, OVER_ROWS, preferred_element_type=F32)
        - row_total[...] * q.astype(F32)
    )
    for j in range(1, group_size):
        block = queries[j][...]
        positive = positive_of(block, items[j][...], scale)
        weights = pair_weights(block, own_items, positive, scale, group_size * pairs).astype(BF16)
        d_item += lax.dot_general(weights, block, OVER_ROWS, preferred_element_type=F32)
    d_proj = jnp.concatenate(
        [d_proj_q[...], through_norm(d_item * scale, proj[pairs:], inv[pairs:])], 0
    )
    d_pre = jnp.concatenate(
        [d_pre_q[...], through_gate(d_proj[pairs:], pre[pairs:], w_out[...])], 0
    )
    core = core_ref[0]
    hid = pre.shape[1]
    cut = hid // 2
    fold = cut * width // hid
    for half, out in ((1 - core, give), (core, keep)):
        grad = lax.dot_general(inputs[half], d_pre, OVER_ROWS, preferred_element_type=F32)
        out[:width] = grad.astype(out.dtype)
        for k in range(hid // width):
            start = pl.multiple_of(half * cut + k * fold, fold)
            grad = lax.dot_general(
                hidden[:, pl.ds(start, fold)], d_proj, OVER_ROWS, preferred_element_type=F32
            )
            out[width:, k * width : (k + 1) * width] = grad.astype(out.dtype)


def call_kernel(kernel, outs, args, flops, scalars=0):
    moved = sum(a.size * a.dtype.itemsize for a in list(args) + list(outs))
    specs = [pl.BlockSpec(memory_space=pltpu.SMEM)] * scalars
    specs += [pl.BlockSpec(memory_space=pltpu.VMEM)] * (len(args) - scalars)
    return pl.pallas_call(
        kernel,
        out_shape=outs,
        in_specs=specs,
        out_specs=[pl.BlockSpec(memory_space=pltpu.VMEM)] * len(outs),
        compiler_params=pltpu.CompilerParams(vmem_limit_bytes=40 * 1024 * 1024),
        cost_estimate=pl.CostEstimate(flops=flops, bytes_accessed=moved, transcendentals=0),
    )(*args)


def backward(embedding, projected, inv_norm, pre_act, hidden, inputs, w_out, group, sizes):
    blk_size = sizes[1]
    nodes, width = embedding.shape
    hid = pre_act.shape[1]
    pairs = nodes // 2
    queries, items = embedding[:pairs], embedding[pairs:]
    all_items = [items] + spread(items, sizes)
    all_queries = [queries] + spread(queries, sizes)
    shape = jax.ShapeDtypeStruct
    scores = 2 * pairs * pairs * width
    tile, row_total, d_proj_q, d_pre_q = call_kernel(
        functools.partial(query_kernel, blk_size),
        [
            shape((pairs, pairs), BF16),
            shape((pairs, 1), F32),
            shape((pairs, width), BF16),
            shape((pairs, hid), BF16),
        ],
        [queries] + all_items + [projected, inv_norm, pre_act, w_out],
        2 * scores * blk_size + 2 * pairs * width * hid,
    )
    rows = width + width // 2
    return call_kernel(
        functools.partial(item_kernel, blk_size),
        [shape((rows, hid), F32), shape((rows, hid), BF16)],
        [jnp.reshape(group % 2, (1,))]
        + all_queries
        + all_items
        + [tile, row_total, projected, inv_norm, pre_act, w_out, d_proj_q, d_pre_q, hidden, inputs],
        2 * scores * blk_size + 2 * pairs * width * hid + 6 * nodes * width * hid,
        scalars=1,
    )


def sum_staged(keep, give, side, group, own, sizes):
    dp_size, blk_size = sizes
    width = keep.shape[1]
    plane = dp_size // 2
    core = group % 2
    across = group // 2

    def unfold(folded):
        return jnp.concatenate(
            [folded[:, k * side : (k + 1) * side] for k in range(width // side)], 0
        )

    def over_core(v, j):
        return exchange(v, sizes, j, 0)

    def over_plane(v, j):
        return exchange(v, sizes, 2 * j, 0)

    def over_blk(v, j):
        return exchange(v, sizes, 0, j)

    total = keep + over_core(give, 1).astype(F32)
    if plane & (plane - 1) == 0 and keep.shape[0] % (8 * plane * blk_size) == 0:
        total = reduce_blocks(total, across, plane, over_plane)
        total = reduce_blocks(total, own, blk_size, over_blk)
        block = total.astype(BF16)
        block = gather_blocks(block, own, blk_size, over_blk)
        block = gather_blocks(block, across, plane, over_plane)
    else:
        halves = jnp.stack([jnp.where(core == c, total, 0.0) for c in range(2)])
        halves = lax.psum(halves, AXES)
        block = jnp.where(core == 0, halves[0], halves[1]).astype(BF16)
    other = over_core(block, 1)
    first = jnp.where(core == 0, block, other)
    second = jnp.where(core == 0, other, block)
    cut = side
    grad_out = jnp.concatenate([unfold(first[cut:]), unfold(second[cut:])], 0)
    return (first[:cut].astype(F32), second[:cut].astype(F32), grad_out.astype(F32))


def on_device(sizes, self_feat, nbr_mask, neighbour_slot, serve_rows, feat_store, w_self, w_nbr, w_out):
    group = lax.axis_index("dp")
    own = lax.axis_index("blk")
    pooled = pooled_mean(nbr_mask, neighbour_slot, serve_rows, feat_store, own, sizes)
    pre_act = jnp.dot(self_feat, w_self, preferred_element_type=F32) + jnp.dot(
        pooled, w_nbr, preferred_element_type=F32
    )
    hidden = (pre_act * jax.nn.sigmoid(pre_act)).astype(BF16)
    projected = jnp.dot(hidden, w_out, preferred_element_type=F32)
    inv_norm = lax.rsqrt(jnp.mean(projected * projected, 1, keepdims=True) + 1e-06)
    embedding = (projected * inv_norm).astype(BF16)
    inputs = jnp.stack([self_feat, pooled])
    keep, give = backward(
        embedding, projected, inv_norm, pre_act, hidden, inputs, w_out, group, sizes
    )
    return sum_staged(keep, give, w_out.shape[1], group, own, sizes)


def solution(mesh):
    sizes = (mesh.shape["dp"], mesh.shape["blk"])
    in_specs = (
        P(("dp", "blk"), None),
        P(("dp", "blk"), None),
        P(("dp", "blk"), None),
        P(("dp", "blk"), None),
        P("blk", None),
        P(),
        P(),
        P(),
    )
    out_specs = (P(), P(), P())

    def body(*arrays):
        return on_device(sizes, *arrays)

    return jax.shard_map(
        body, mesh=mesh, in_specs=in_specs, out_specs=out_specs, check_vma=False
    )
```

```python
import functools

import jax
import jax.numpy as jnp
from jax import lax
from jax.experimental import pallas as pl
from jax.experimental.pallas import tpu as pltpu
from jax.sharding import PartitionSpec as P

MARGIN = 0.5
AXES = ("dp", "blk")
BF16 = jnp.bfloat16
F32 = jnp.float32
OVER_ROWS = (((0,), (0,)), ((), ()))
LAST_DIMS = (((1,), (1,)), ((), ()))


def exchange(value, sizes, flip_dp, flip_blk):
    dp_size, blk_size = sizes
    pairs = [
        (g * blk_size + b, (g ^ flip_dp) * blk_size + (b ^ flip_blk))
        for g in range(dp_size)
        for b in range(blk_size)
    ]
    return lax.ppermute(value, AXES, pairs)


def block_of(array, index, count):
    rows = array.shape[0] // count
    return lax.dynamic_slice_in_dim(array, index * rows, rows, 0)


def in_order(parts, own):
    ordered = []
    for place in range(len(parts)):
        block = parts[place]
        for own_value in range(1, len(parts)):
            block = jnp.where(own == own_value, parts[place ^ own_value], block)
        ordered.append(block)
    return jnp.concatenate(ordered, 0)


def reduce_blocks(array, own, count, send):
    arrived = [send(block_of(array, own ^ j, count).astype(BF16), j) for j in range(1, count)]
    total = block_of(array, own, count)
    for part in arrived:
        total = total + part.astype(F32)
    return total


def gather_blocks(block, own, count, send):
    return in_order([block] + [send(block, j) for j in range(1, count)], own)


def node_of_arrival(neighbour_slot, valid, count):
    slots = neighbour_slot.shape[1]
    low = 128
    node = lax.broadcasted_iota(jnp.int32, (1, slots), 1) // (slots // valid.shape[0])
    flat_valid = valid.reshape(1, slots)
    high_hot = lax.broadcasted_iota(jnp.int32, (slots // low, slots), 0) == neighbour_slot // low
    low_hot = lax.broadcasted_iota(jnp.int32, (low, slots), 0) == neighbour_slot % low
    upper = ((node // 16 + 1) * flat_valid).astype(F32)
    lower = ((node % 16) * flat_valid).astype(F32)
    codes = jnp.concatenate(
        [jnp.where(low_hot, upper, 0.0), jnp.where(low_hot, lower, 0.0)], 0
    ).astype(BF16)
    found = lax.dot_general(
        high_hot.astype(BF16), codes, (((1,), (1,)), ((), ())), preferred_element_type=F32
    )
    found = found.astype(jnp.int32)
    return ((found[:, :low] - 1) * 16 + found[:, low:]).reshape(count, slots // count)


def call_kernel(kernel, outs, args, flops=0, scalars=0, scratch=()):
    moved = sum(a.size * a.dtype.itemsize for a in list(args) + list(outs)) if flops else 0
    specs = [pl.BlockSpec(memory_space=pltpu.SMEM)] * scalars
    specs += [pl.BlockSpec(memory_space=pltpu.VMEM)] * (len(args) - scalars)
    return pl.pallas_call(
        kernel,
        out_shape=outs,
        in_specs=specs,
        out_specs=[pl.BlockSpec(memory_space=pltpu.VMEM)] * len(outs),
        scratch_shapes=list(scratch),
        compiler_params=pltpu.CompilerParams(vmem_limit_bytes=24 * 1024 * 1024),
        cost_estimate=pl.CostEstimate(flops=flops, bytes_accessed=moved, transcendentals=0),
    )(*args)


def split_kernel(store, left, right):
    rows, side = left.shape
    step = rows // 16

    def some_rows(i, carry):
        at = pl.ds(pl.multiple_of(i * step, step), step)
        block = store[at, :].astype(F32)
        left[at, :] = block[:, :side]
        right[at, :] = block[:, side:]
        return carry

    lax.fori_loop(0, 16, some_rows, 0)


def partial_kernel(requester, serve_rows, node_at, left, right, out, got_left, got_right):
    count = node_at.shape[1]
    first = requester[0] * count

    def some_rows(i, carry):
        base = i * 32
        wanted = [serve_rows[first + base + u] for u in range(32)]
        for tile in range(0, 32, 8):
            at = pl.ds(pl.multiple_of(base + tile, 8), 8)
            to_left, to_right = got_left.at[at, :], got_right.at[at, :]
            for u in range(8):
                row = pl.ds(wanted[tile + u], 1)
                to_left[u : u + 1, :] = left[row, :]
                to_right[u : u + 1, :] = right[row, :]
        return carry

    lax.fori_loop(0, count // 32, some_rows, 0)
    nodes = lax.broadcasted_iota(jnp.int32, (out.shape[0], count), 0)
    pick = (nodes == node_at[...]).astype(BF16)
    rows = jnp.concatenate([got_left[...], got_right[...]], 1).astype(BF16)
    out[...] = jnp.dot(pick, rows, preferred_element_type=F32).astype(out.dtype)


def pooled_mean(nbr_mask, neighbour_slot, serve_rows, feat_store, own, sizes):
    blk_size = sizes[1]
    nodes = nbr_mask.shape[0]
    first_col = lax.broadcasted_iota(jnp.int32, nbr_mask.shape, 1) == 0
    valid = jnp.where(first_col, 1, nbr_mask)
    live_count = jnp.sum(valid.astype(F32), 1, keepdims=True)
    node_at = node_of_arrival(neighbour_slot, valid, blk_size)
    order = list(range(blk_size - 1, 0, -1))
    wanted = {
        j: exchange(block_of(node_at, own ^ j, blk_size), sizes, 0, j) for j in order
    }
    wanted = dict(zip(wanted, lax.optimization_barrier(tuple(wanted.values()))))
    wanted[0] = block_of(node_at, own, blk_size)
    width = feat_store.shape[1]
    cap = serve_rows.shape[1]
    shape = jax.ShapeDtypeStruct
    halves = call_kernel(
        split_kernel, [shape((feat_store.shape[0], width // 2), F32)] * 2, [feat_store]
    )
    served = serve_rows.reshape(-1)
    parts = {}
    for j in order + [0]:
        (parts[j],) = call_kernel(
            partial_kernel,
            [shape((nodes, width), BF16 if j % 2 else F32)],
            [jnp.reshape(own ^ j, (1,)), served, wanted[j]] + list(halves),
            scalars=2,
            scratch=[pltpu.VMEM((cap, width // 2), F32)] * 2,
        )
        if j:
            served, parts[j] = lax.optimization_barrier((served, parts[j]))
    for_own = []
    bit = 1
    while bit < blk_size:
        for j in [j for j in order if j & bit and j in parts]:
            arrived = exchange(parts.pop(j).astype(BF16), sizes, 0, bit)
            if j == bit:
                for_own.append(arrived)
            else:
                parts[j ^ bit] = parts[j ^ bit] + arrived.astype(F32)
        bit *= 2
    total = parts[0]
    for part in for_own:
        total = total + part.astype(F32)
    return (total / live_count).astype(BF16)


def spread(block, sizes):
    blk_size = sizes[1]
    known = {0: block}
    bit = blk_size // 2
    while bit:
        known.update({j ^ bit: exchange(v, sizes, 0, bit) for j, v in list(known.items())})
        bit //= 2
    return [known[j] for j in range(1, blk_size)]


def pair_weights(q, i, positive, scale, columns):
    scores = lax.dot_general(q, i, LAST_DIMS, preferred_element_type=F32)
    return jax.nn.sigmoid(scores * scale - positive + MARGIN) / columns


def positive_of(q, i, scale):
    return jnp.sum(q.astype(F32) * i.astype(F32), 1, keepdims=True) * scale


def through_norm(d_embed, proj, inv):
    interior = jnp.mean(d_embed * proj, 1, keepdims=True)
    return (inv * d_embed - proj * inv**3 * interior).astype(BF16)


def through_gate(d_proj, pre, w_out):
    d_hidden = lax.dot_general(d_proj, w_out, LAST_DIMS, preferred_element_type=F32)
    sig = jax.nn.sigmoid(pre)
    return (d_hidden * sig * (1.0 + pre * (1.0 - sig))).astype(BF16)


def query_kernel(group_size, *refs):
    queries, items = refs[0], refs[1 : 1 + group_size]
    proj, inv, pre, w_out, tile, row_total, d_proj, d_pre = refs[1 + group_size :]
    q, own_items = queries[...], items[0][...]
    pairs, width = q.shape
    scale = width ** (-0.5)
    positive = positive_of(q, own_items, scale)
    total = jnp.zeros((pairs, 1), F32)
    d_query = jnp.zeros((pairs, width), F32)
    for j in range(group_size):
        block = items[j][...]
        weights = pair_weights(q, block, positive, scale, group_size * pairs)
        total += jnp.sum(weights, 1, keepdims=True)
        rounded = weights.astype(BF16)
        if j == 0:
            tile[...] = rounded
        d_query += jnp.dot(rounded, block, preferred_element_type=F32)
    row_total[...] = total
    d_query = (d_query - total * own_items.astype(F32)) * scale
    d_p = through_norm(d_query, proj[:pairs], inv[:pairs])
    d_proj[...] = d_p
    d_pre[...] = through_gate(d_p, pre[:pairs], w_out[...])


def item_kernel(group_size, core_ref, *refs):
    queries, items = refs[:group_size], refs[group_size : 2 * group_size]
    (tile, row_total, proj, inv, pre, w_out, d_proj_q, d_pre_q, hidden, feat, pooled, keep, give) = refs[
        2 * group_size :
    ]
    own_items, q = items[0][...], queries[0][...]
    pairs, width = q.shape
    scale = width ** (-0.5)
    d_item = (
        lax.dot_general(tile[...], q, OVER_ROWS, preferred_element_type=F32)
        - row_total[...] * q.astype(F32)
    )
    for j in range(1, group_size):
        block = queries[j][...]
        positive = positive_of(block, items[j][...], scale)
        weights = pair_weights(block, own_items, positive, scale, group_size * pairs).astype(BF16)
        d_item += lax.dot_general(weights, block, OVER_ROWS, preferred_element_type=F32)
    d_proj = jnp.concatenate(
        [d_proj_q[...], through_norm(d_item * scale, proj[pairs:], inv[pairs:])], 0
    )
    d_pre = jnp.concatenate(
        [d_pre_q[...], through_gate(d_proj[pairs:], pre[pairs:], w_out[...])], 0
    )
    core = core_ref[0]
    hid = pre.shape[1]
    cut = hid // 2
    fold = cut * width // hid
    for half, out in ((1 - core, give), (core, keep)):
        rows = jnp.where(half == 0, feat[...], pooled[...])
        grad = lax.dot_general(rows, d_pre, OVER_ROWS, preferred_element_type=F32)
        out[:width] = grad.astype(out.dtype)
        for k in range(hid // width):
            start = pl.multiple_of(half * cut + k * fold, fold)
            grad = lax.dot_general(
                hidden[:, pl.ds(start, fold)], d_proj, OVER_ROWS, preferred_element_type=F32
            )
            out[width:, k * width : (k + 1) * width] = grad.astype(out.dtype)


def backward(queries, items, projected, inv_norm, pre_act, hidden, feat, pooled, w_out, group, sizes):
    blk_size = sizes[1]
    nodes, hid = pre_act.shape
    pairs, width = queries.shape
    all_items = [items] + spread(items, sizes)
    all_queries = [queries] + spread(queries, sizes)
    shape = jax.ShapeDtypeStruct
    scores = 2 * pairs * pairs * width
    tile, row_total, d_proj_q, d_pre_q = call_kernel(
        functools.partial(query_kernel, blk_size),
        [
            shape((pairs, pairs), BF16),
            shape((pairs, 1), F32),
            shape((pairs, width), BF16),
            shape((pairs, hid), BF16),
        ],
        [queries] + all_items + [projected, inv_norm, pre_act, w_out],
        2 * scores * blk_size + 2 * pairs * width * hid,
    )
    rows = width + width // 2
    return call_kernel(
        functools.partial(item_kernel, blk_size),
        [shape((rows, hid), F32), shape((rows, hid), BF16)],
        [jnp.reshape(group % 2, (1,))]
        + all_queries
        + all_items
        + [tile, row_total, projected, inv_norm, pre_act, w_out, d_proj_q, d_pre_q]
        + [hidden, feat, pooled],
        2 * scores * blk_size + 2 * pairs * width * hid + 6 * nodes * width * hid,
        scalars=1,
    )


def sum_staged(keep, give, side, group, own, sizes):
    dp_size, blk_size = sizes
    width = keep.shape[1]
    plane = dp_size // 2
    core = group % 2
    across = group // 2

    def unfold(folded):
        return jnp.concatenate(
            [folded[:, k * side : (k + 1) * side] for k in range(width // side)], 0
        )

    def over_core(v, j):
        return exchange(v, sizes, j, 0)

    def over_plane(v, j):
        return exchange(v, sizes, 2 * j, 0)

    def over_blk(v, j):
        return exchange(v, sizes, 0, j)

    total = keep + over_core(give, 1).astype(F32)
    if plane & (plane - 1) == 0 and keep.shape[0] % (8 * plane * blk_size) == 0:
        total = reduce_blocks(total, across, plane, over_plane)
        total = reduce_blocks(total, own, blk_size, over_blk)
        block = total.astype(BF16)
        block = gather_blocks(block, own, blk_size, over_blk)
        block = gather_blocks(block, across, plane, over_plane)
    else:
        halves = jnp.stack([jnp.where(core == c, total, 0.0) for c in range(2)])
        halves = lax.psum(halves, AXES)
        block = jnp.where(core == 0, halves[0], halves[1]).astype(BF16)
    other = over_core(block, 1)
    first = jnp.where(core == 0, block, other)
    second = jnp.where(core == 0, other, block)
    cut = side
    grad_out = jnp.concatenate([unfold(first[cut:]), unfold(second[cut:])], 0)
    return (first[:cut].astype(F32), second[:cut].astype(F32), grad_out.astype(F32))


def on_device(sizes, self_feat, nbr_mask, neighbour_slot, serve_rows, feat_store, w_self, w_nbr, w_out):
    group = lax.axis_index("dp")
    own = lax.axis_index("blk")
    pooled = pooled_mean(nbr_mask, neighbour_slot, serve_rows, feat_store, own, sizes)
    pre_act = jnp.dot(self_feat, w_self, preferred_element_type=F32) + jnp.dot(
        pooled, w_nbr, preferred_element_type=F32
    )
    hidden = (pre_act * jax.nn.sigmoid(pre_act)).astype(BF16)
    projected = jnp.dot(hidden, w_out, preferred_element_type=F32)
    inv_norm = lax.rsqrt(jnp.mean(projected * projected, 1, keepdims=True) + 1e-06)
    embedding = (projected * inv_norm).astype(BF16)
    pairs = embedding.shape[0] // 2
    queries, items = embedding[:pairs], embedding[pairs:]
    keep, give = backward(
        queries, items, projected, inv_norm, pre_act, hidden, self_feat, pooled, w_out, group, sizes
    )
    return sum_staged(keep, give, w_out.shape[1], group, own, sizes)


def solution(mesh):
    sizes = (mesh.shape["dp"], mesh.shape["blk"])
    in_specs = (
        P(("dp", "blk"), None),
        P(("dp", "blk"), None),
        P(("dp", "blk"), None),
        P(("dp", "blk"), None),
        P("blk", None),
        P(),
        P(),
        P(),
    )
    out_specs = (P(), P(), P())

    def body(*arrays):
        return on_device(sizes, *arrays)

    return jax.shard_map(
        body, mesh=mesh, in_specs=in_specs, out_specs=out_specs, check_vma=False
    )
```

```python
import functools

import jax
import jax.numpy as jnp
from jax import lax
from jax.experimental import pallas as pl
from jax.experimental.layout import Layout, with_layout_constraint
from jax.experimental.pallas import tpu as pltpu
from jax.sharding import PartitionSpec as P

MARGIN = 0.5
AXES = ("dp", "blk")
BF16 = jnp.bfloat16
F32 = jnp.float32
OVER_ROWS = (((0,), (0,)), ((), ()))
LAST_DIMS = (((1,), (1,)), ((), ()))


def exchange(value, sizes, flip_dp, flip_blk):
    dp_size, blk_size = sizes
    pairs = [
        (g * blk_size + b, (g ^ flip_dp) * blk_size + (b ^ flip_blk))
        for g in range(dp_size)
        for b in range(blk_size)
    ]
    return lax.ppermute(value, AXES, pairs)


def block_of(array, index, count):
    rows = array.shape[0] // count
    return lax.dynamic_slice_in_dim(array, index * rows, rows, 0)


def in_order(parts, own):
    ordered = []
    for place in range(len(parts)):
        block = parts[place]
        for own_value in range(1, len(parts)):
            block = jnp.where(own == own_value, parts[place ^ own_value], block)
        ordered.append(block)
    return jnp.concatenate(ordered, 0)


def reduce_blocks(array, own, count, send):
    arrived = [send(block_of(array, own ^ j, count).astype(BF16), j) for j in range(1, count)]
    total = block_of(array, own, count)
    for part in arrived:
        total = total + part.astype(F32)
    return total


def gather_blocks(block, own, count, send):
    return in_order([block] + [send(block, j) for j in range(1, count)], own)


def node_of_arrival(neighbour_slot, valid, count):
    slots = neighbour_slot.shape[1]
    low = 128
    node = lax.broadcasted_iota(jnp.int32, (1, slots), 1) // (slots // valid.shape[0])
    flat_valid = valid.reshape(1, slots)
    high_hot = lax.broadcasted_iota(jnp.int32, (slots // low, slots), 0) == neighbour_slot // low
    low_hot = lax.broadcasted_iota(jnp.int32, (low, slots), 0) == neighbour_slot % low
    upper = ((node // 16 + 1) * flat_valid).astype(F32)
    lower = ((node % 16) * flat_valid).astype(F32)
    codes = jnp.concatenate(
        [jnp.where(low_hot, upper, 0.0), jnp.where(low_hot, lower, 0.0)], 0
    ).astype(BF16)
    found = lax.dot_general(
        high_hot.astype(BF16), codes, (((1,), (1,)), ((), ())), preferred_element_type=F32
    )
    found = found.astype(jnp.int32)
    return ((found[:, :low] - 1) * 16 + found[:, low:]).reshape(count, slots // count)


SPACES = {"s": pltpu.SMEM, "v": pltpu.VMEM, "a": pl.ANY}


def call_kernel(kernel, outs, args, flops=0, spaces="", outs_in="", scratch=()):
    moved = sum(a.size * a.dtype.itemsize for a in list(args) + list(outs)) if flops else 0
    return pl.pallas_call(
        kernel,
        out_shape=outs,
        in_specs=[pl.BlockSpec(memory_space=SPACES[c]) for c in spaces.ljust(len(args), "v")],
        out_specs=[pl.BlockSpec(memory_space=SPACES[c]) for c in outs_in.ljust(len(outs), "v")],
        scratch_shapes=list(scratch),
        compiler_params=pltpu.CompilerParams(vmem_limit_bytes=24 * 1024 * 1024),
        cost_estimate=pl.CostEstimate(flops=flops, bytes_accessed=moved, transcendentals=0),
    )(*args)


def split_kernel(store, left, right):
    rows, side = left.shape
    step = rows // 16

    def some_rows(i, carry):
        at = pl.ds(pl.multiple_of(i * step, step), step)
        block = store[at, :].astype(F32)
        left[at, :] = block[:, :side]
        right[at, :] = block[:, side:]
        return carry

    lax.fori_loop(0, 16, some_rows, 0)


def partial_kernel(requester, serve_rows, node_at, left, right, out, got_left, got_right):
    count = node_at.shape[1]
    first = requester[0] * count

    def some_rows(i, carry):
        base = i * 32
        wanted = [serve_rows[first + base + u] for u in range(32)]
        for tile in range(0, 32, 8):
            at = pl.ds(pl.multiple_of(base + tile, 8), 8)
            to_left, to_right = got_left.at[at, :], got_right.at[at, :]
            for u in range(8):
                row = pl.ds(wanted[tile + u], 1)
                to_left[u : u + 1, :] = left[row, :]
                to_right[u : u + 1, :] = right[row, :]
        return carry

    lax.fori_loop(0, count // 32, some_rows, 0)
    nodes = lax.broadcasted_iota(jnp.int32, (out.shape[0], count), 0)
    pick = (nodes == node_at[...]).astype(BF16)
    rows = jnp.concatenate([got_left[...], got_right[...]], 1).astype(BF16)
    out[...] = jnp.dot(pick, rows, preferred_element_type=F32).astype(out.dtype)


def pooled_mean(nbr_mask, neighbour_slot, serve_rows, feat_store, own, sizes):
    blk_size = sizes[1]
    nodes = nbr_mask.shape[0]
    first_col = lax.broadcasted_iota(jnp.int32, nbr_mask.shape, 1) == 0
    valid = jnp.where(first_col, 1, nbr_mask)
    live_count = jnp.sum(valid.astype(F32), 1, keepdims=True)
    node_at = node_of_arrival(neighbour_slot, valid, blk_size)
    order = list(range(blk_size - 1, 0, -1))
    wanted = {
        j: exchange(block_of(node_at, own ^ j, blk_size), sizes, 0, j) for j in order
    }
    wanted = dict(zip(wanted, lax.optimization_barrier(tuple(wanted.values()))))
    wanted[0] = block_of(node_at, own, blk_size)
    width = feat_store.shape[1]
    cap = serve_rows.shape[1]
    shape = jax.ShapeDtypeStruct
    halves = call_kernel(
        split_kernel, [shape((feat_store.shape[0], width // 2), F32)] * 2, [feat_store]
    )
    served = serve_rows.reshape(-1)
    parts = {}
    for j in order + [0]:
        (parts[j],) = call_kernel(
            partial_kernel,
            [shape((nodes, width), BF16 if j % 2 else F32)],
            [jnp.reshape(own ^ j, (1,)), served, wanted[j]] + list(halves),
            spaces="ss",
            scratch=[pltpu.VMEM((cap, width // 2), F32)] * 2,
        )
        if j:
            served, parts[j] = lax.optimization_barrier((served, parts[j]))
    for_own = []
    bit = 1
    while bit < blk_size:
        for j in [j for j in order if j & bit and j in parts]:
            arrived = exchange(parts.pop(j).astype(BF16), sizes, 0, bit)
            if j == bit:
                for_own.append(arrived)
            else:
                parts[j ^ bit] = parts[j ^ bit] + arrived.astype(F32)
        bit *= 2
    total = parts[0]
    for part in for_own:
        total = total + part.astype(F32)
    return (total / live_count).astype(BF16)


def spread(block, sizes):
    blk_size = sizes[1]
    known = {0: block}
    bit = blk_size // 2
    while bit:
        known.update({j ^ bit: exchange(v, sizes, 0, bit) for j, v in list(known.items())})
        bit //= 2
    return [known[j] for j in range(1, blk_size)]


def pair_weights(q, i, positive, scale, columns):
    scores = lax.dot_general(q, i, LAST_DIMS, preferred_element_type=F32)
    return jax.nn.sigmoid(scores * scale - positive + MARGIN) / columns


def positive_of(q, i, scale):
    return jnp.sum(q.astype(F32) * i.astype(F32), 1, keepdims=True) * scale


def through_norm(d_embed, proj, inv):
    interior = jnp.mean(d_embed * proj, 1, keepdims=True)
    return (inv * d_embed - proj * inv**3 * interior).astype(BF16)


def through_gate(d_proj, pre, w_out):
    d_hidden = lax.dot_general(d_proj, w_out, LAST_DIMS, preferred_element_type=F32)
    sig = jax.nn.sigmoid(pre)
    return (d_hidden * sig * (1.0 + pre * (1.0 - sig))).astype(BF16)


def query_kernel(group_size, *refs):
    queries, items = refs[0], refs[1 : 1 + group_size]
    proj, inv, pre, w_out, tile, row_total, d_proj, d_pre = refs[1 + group_size :]
    q, own_items = queries[...], items[0][...]
    pairs, width = q.shape
    scale = width ** (-0.5)
    positive = positive_of(q, own_items, scale)
    total = jnp.zeros((pairs, 1), F32)
    d_query = jnp.zeros((pairs, width), F32)
    for j in range(group_size):
        block = items[j][...]
        weights = pair_weights(q, block, positive, scale, group_size * pairs)
        total += jnp.sum(weights, 1, keepdims=True)
        rounded = weights.astype(BF16)
        if j == 0:
            tile[...] = rounded
        d_query += jnp.dot(rounded, block, preferred_element_type=F32)
    row_total[...] = total
    d_query = (d_query - total * own_items.astype(F32)) * scale
    d_p = through_norm(d_query, proj[:pairs], inv[:pairs])
    d_proj[...] = d_p
    d_pre[...] = through_gate(d_p, pre[:pairs], w_out[...])


def item_kernel(group_size, core_ref, *refs):
    queries, items = refs[:group_size], refs[group_size : 2 * group_size]
    (tile, row_total, proj, inv, pre, w_out, d_proj_q, d_pre_q, hidden, feat, pooled, keep, give) = refs[
        2 * group_size :
    ]
    own_items, q = items[0][...], queries[0][...]
    pairs, width = q.shape
    scale = width ** (-0.5)
    d_item = (
        lax.dot_general(tile[...], q, OVER_ROWS, preferred_element_type=F32)
        - row_total[...] * q.astype(F32)
    )
    for j in range(1, group_size):
        block = queries[j][...]
        positive = positive_of(block, items[j][...], scale)
        weights = pair_weights(block, own_items, positive, scale, group_size * pairs).astype(BF16)
        d_item += lax.dot_general(weights, block, OVER_ROWS, preferred_element_type=F32)
    d_proj = jnp.concatenate(
        [d_proj_q[...], through_norm(d_item * scale, proj[pairs:], inv[pairs:])], 0
    )
    d_pre = jnp.concatenate(
        [d_pre_q[...], through_gate(d_proj[pairs:], pre[pairs:], w_out[...])], 0
    )
    core = core_ref[0]
    hid = pre.shape[1]
    cut = hid // 2
    fold = cut * width // hid
    for half, out in ((1 - core, give), (core, keep)):
        rows = jnp.where(half == 0, feat[...], pooled[...])
        grad = lax.dot_general(rows, d_pre, OVER_ROWS, preferred_element_type=F32)
        out[:width] = grad.astype(out.dtype)
        for k in range(hid // width):
            start = pl.multiple_of(half * cut + k * fold, fold)
            grad = lax.dot_general(
                hidden[:, pl.ds(start, fold)], d_proj, OVER_ROWS, preferred_element_type=F32
            )
            out[width:, k * width : (k + 1) * width] = grad.astype(out.dtype)


def cut_kernel(place, keep, arrived, *refs):
    pieces = refs
    rows = pieces[0].shape[0]
    for j, piece in enumerate(pieces):
        at = pl.ds(pl.multiple_of((place[0] ^ j) * rows, rows), rows)
        piece[...] = (keep[at, :].astype(F32) + arrived[at, :].astype(F32)).astype(piece.dtype)


def finish_kernel(place, block, other, *refs):
    outs, held, done = refs[:3], refs[3:6], refs[6]
    hid, width = held[2].shape
    cut = held[0].shape[0]
    fold = block.shape[0] - cut
    own = place[0]
    copies = [pltpu.make_async_copy(held[n], outs[n], done.at[n]) for n in range(3)]

    def half(index, at):
        return jnp.where(own == index, block[at], other[at]).astype(F32)

    for index in range(2):
        held[index][...] = half(index, (slice(0, cut), slice(None)))
        copies[index].start()
    for index in range(2):
        for k in range(hid // width):
            at = (slice(cut, cut + fold), slice(k * width, (k + 1) * width))
            start = index * (hid // 2) + k * fold
            held[2][start : start + fold, :] = half(index, at)
    copies[2].start()
    for copy in copies:
        copy.wait()


def backward(queries, items, projected, inv_norm, pre_act, hidden, feat, pooled, w_out, group, own, sizes):
    blk_size = sizes[1]
    nodes, hid = pre_act.shape
    pairs, width = queries.shape
    all_items = [items] + spread(items, sizes)
    all_queries = [queries] + spread(queries, sizes)
    shape = jax.ShapeDtypeStruct
    scores = 2 * pairs * pairs * width
    tile, row_total, d_proj_q, d_pre_q = call_kernel(
        functools.partial(query_kernel, blk_size),
        [
            shape((pairs, pairs), BF16),
            shape((pairs, 1), F32),
            shape((pairs, width), BF16),
            shape((pairs, hid), BF16),
        ],
        [queries] + all_items + [projected, inv_norm, pre_act, w_out],
        2 * scores * blk_size + 2 * pairs * width * hid,
    )
    rows = width + width // 2
    plane = sizes[0] // 2
    core = group % 2
    across = group // 2
    if plane & (plane - 1) or rows % (16 * plane) or rows % (8 * plane * blk_size):
        plane = 1
    keep, give = call_kernel(
        functools.partial(item_kernel, blk_size),
        [shape((rows, hid), F32), shape((rows, hid), BF16)],
        [jnp.reshape(core, (1,))]
        + all_queries
        + all_items
        + [tile, row_total, projected, inv_norm, pre_act, w_out, d_proj_q, d_pre_q]
        + [hidden, feat, pooled],
        2 * scores * blk_size + 2 * pairs * width * hid + 6 * nodes * width * hid,
        spaces="s",
    )
    pieces = call_kernel(
        cut_kernel,
        [shape((rows // plane, hid), BF16 if j else F32) for j in range(plane)],
        [jnp.reshape(across % plane, (1,)), keep, exchange(give, sizes, 1, 0)],
        spaces="s",
    )
    return sum_staged(pieces, core, across, own, sizes)


def sum_staged(pieces, core, across, own, sizes):
    blk_size = sizes[1]
    plane = len(pieces)

    def over_core(v, j):
        return exchange(v, sizes, j, 0)

    def over_plane(v, j):
        return exchange(v, sizes, 2 * j, 0)

    def over_blk(v, j):
        return exchange(v, sizes, 0, j)

    total = pieces[0]
    if plane > 1:
        for j in range(1, plane):
            total = total + over_plane(pieces[j], j).astype(F32)
        total = reduce_blocks(total, own, blk_size, over_blk)
        block = total.astype(BF16)
        block = gather_blocks(block, own, blk_size, over_blk)
        block = gather_blocks(block, across, plane, over_plane)
    else:
        halves = jnp.stack([jnp.where(core == c, total, 0.0) for c in range(2)])
        halves = lax.psum(halves, AXES)
        block = jnp.where(core == 0, halves[0], halves[1]).astype(BF16)
    other = over_core(block, 1)
    rows, hid = block.shape
    width = rows * 2 // 3
    outs = [(width, hid), (width, hid), (hid, width)]
    return tuple(
        call_kernel(
            finish_kernel,
            [jax.ShapeDtypeStruct(o, F32) for o in outs],
            [jnp.reshape(core, (1,)), block, other],
            spaces="s",
            outs_in="aaa",
            scratch=[pltpu.VMEM(o, F32) for o in outs] + [pltpu.SemaphoreType.DMA((3,))],
        )
    )


def on_device(sizes, self_feat, nbr_mask, neighbour_slot, serve_rows, feat_store, w_self, w_nbr, w_out):
    group = lax.axis_index("dp")
    own = lax.axis_index("blk")
    pooled = pooled_mean(nbr_mask, neighbour_slot, serve_rows, feat_store, own, sizes)
    pre_act = jnp.dot(self_feat, w_self, preferred_element_type=F32) + jnp.dot(
        pooled, w_nbr, preferred_element_type=F32
    )
    hidden = (pre_act * jax.nn.sigmoid(pre_act)).astype(BF16)
    projected = with_layout_constraint(
        jnp.dot(hidden, w_out, preferred_element_type=F32), Layout((0, 1))
    )
    inv_norm = lax.rsqrt(jnp.mean(projected * projected, 1, keepdims=True) + 1e-06)
    embedding = (projected * inv_norm).astype(BF16)
    pairs = embedding.shape[0] // 2
    queries, items = embedding[:pairs], embedding[pairs:]
    return backward(
        queries, items, projected, inv_norm, pre_act, hidden, self_feat, pooled, w_out, group, own, sizes
    )


def solution(mesh):
    sizes = (mesh.shape["dp"], mesh.shape["blk"])
    in_specs = (
        P(("dp", "blk"), None),
        P(("dp", "blk"), None),
        P(("dp", "blk"), None),
        P(("dp", "blk"), None),
        P("blk", None),
        P(),
        P(),
        P(),
    )
    out_specs = (P(), P(), P())

    def body(*arrays):
        return on_device(sizes, *arrays)

    return jax.shard_map(
        body, mesh=mesh, in_specs=in_specs, out_specs=out_specs, check_vma=False
    )
```

```python
import functools

import jax
import jax.numpy as jnp
from jax import lax
from jax.experimental import pallas as pl
from jax.experimental.layout import Layout, with_layout_constraint
from jax.experimental.pallas import tpu as pltpu
from jax.sharding import PartitionSpec as P

MARGIN = 0.5
AXES = ("dp", "blk")
BF16 = jnp.bfloat16
F32 = jnp.float32
OVER_ROWS = (((0,), (0,)), ((), ()))
LAST_DIMS = (((1,), (1,)), ((), ()))


def exchange(value, sizes, flip_dp, flip_blk):
    dp_size, blk_size = sizes
    pairs = [
        (g * blk_size + b, (g ^ flip_dp) * blk_size + (b ^ flip_blk))
        for g in range(dp_size)
        for b in range(blk_size)
    ]
    return lax.ppermute(value, AXES, pairs)


def block_of(array, index, count):
    rows = array.shape[0] // count
    return lax.dynamic_slice_in_dim(array, index * rows, rows, 0)


def in_order(parts, own):
    ordered = []
    for place in range(len(parts)):
        block = parts[place]
        for own_value in range(1, len(parts)):
            block = jnp.where(own == own_value, parts[place ^ own_value], block)
        ordered.append(block)
    return jnp.concatenate(ordered, 0)


def reduce_blocks(array, own, count, send):
    arrived = [send(block_of(array, own ^ j, count).astype(BF16), j) for j in range(1, count)]
    total = block_of(array, own, count)
    for part in arrived:
        total = total + part.astype(F32)
    return total


def gather_blocks(block, own, count, send):
    return in_order([block] + [send(block, j) for j in range(1, count)], own)


def node_of_arrival(neighbour_slot, valid, count):
    slots = neighbour_slot.shape[1]
    low = 128
    node = lax.broadcasted_iota(jnp.int32, (1, slots), 1) // (slots // valid.shape[0])
    flat_valid = valid.reshape(1, slots)
    high_hot = lax.broadcasted_iota(jnp.int32, (slots // low, slots), 0) == neighbour_slot // low
    low_hot = lax.broadcasted_iota(jnp.int32, (low, slots), 0) == neighbour_slot % low
    upper = ((node // 16 + 1) * flat_valid).astype(F32)
    lower = ((node % 16) * flat_valid).astype(F32)
    codes = jnp.concatenate(
        [jnp.where(low_hot, upper, 0.0), jnp.where(low_hot, lower, 0.0)], 0
    ).astype(BF16)
    found = lax.dot_general(
        high_hot.astype(BF16), codes, (((1,), (1,)), ((), ())), preferred_element_type=F32
    )
    found = found.astype(jnp.int32)
    return ((found[:, :low] - 1) * 16 + found[:, low:]).reshape(count, slots // count)


SPACES = {"s": pltpu.SMEM, "v": pltpu.VMEM, "a": pl.ANY}


def call_kernel(kernel, outs, args, flops=0, spaces="", outs_in="", scratch=()):
    moved = sum(a.size * a.dtype.itemsize for a in list(args) + list(outs)) if flops else 0
    return pl.pallas_call(
        kernel,
        out_shape=outs,
        in_specs=[pl.BlockSpec(memory_space=SPACES[c]) for c in spaces.ljust(len(args), "v")],
        out_specs=[pl.BlockSpec(memory_space=SPACES[c]) for c in outs_in.ljust(len(outs), "v")],
        scratch_shapes=list(scratch),
        compiler_params=pltpu.CompilerParams(vmem_limit_bytes=24 * 1024 * 1024),
        cost_estimate=pl.CostEstimate(flops=flops, bytes_accessed=moved, transcendentals=0),
    )(*args)


def split_kernel(store, left, right):
    rows, side = left.shape
    step = rows // 16

    def some_rows(i, carry):
        at = pl.ds(pl.multiple_of(i * step, step), step)
        block = store[at, :].astype(F32)
        left[at, :] = block[:, :side]
        right[at, :] = block[:, side:]
        return carry

    lax.fori_loop(0, 16, some_rows, 0)


def partial_kernel(requester, serve_rows, node_at, left, right, out, got_left, got_right):
    count = node_at.shape[1]
    first = requester[0] * count

    def some_rows(i, carry):
        base = i * 32
        wanted = [serve_rows[first + base + u] for u in range(32)]
        for tile in range(0, 32, 8):
            at = pl.ds(pl.multiple_of(base + tile, 8), 8)
            to_left, to_right = got_left.at[at, :], got_right.at[at, :]
            for u in range(8):
                row = pl.ds(wanted[tile + u], 1)
                to_left[u : u + 1, :] = left[row, :]
                to_right[u : u + 1, :] = right[row, :]
        return carry

    lax.fori_loop(0, count // 32, some_rows, 0)
    nodes = lax.broadcasted_iota(jnp.int32, (out.shape[0], count), 0)
    pick = (nodes == node_at[...]).astype(BF16)
    rows = jnp.concatenate([got_left[...], got_right[...]], 1).astype(BF16)
    out[...] = jnp.dot(pick, rows, preferred_element_type=F32).astype(out.dtype)


def pooled_sums(nbr_mask, neighbour_slot, serve_rows, feat_store, own, sizes):
    blk_size = sizes[1]
    nodes = nbr_mask.shape[0]
    first_col = lax.broadcasted_iota(jnp.int32, nbr_mask.shape, 1) == 0
    valid = jnp.where(first_col, 1, nbr_mask)
    live_count = jnp.sum(valid.astype(F32), 1, keepdims=True)
    node_at = node_of_arrival(neighbour_slot, valid, blk_size)
    order = list(range(blk_size - 1, 0, -1))
    wanted = {
        j: exchange(block_of(node_at, own ^ j, blk_size), sizes, 0, j) for j in order
    }
    wanted = dict(zip(wanted, lax.optimization_barrier(tuple(wanted.values()))))
    wanted[0] = block_of(node_at, own, blk_size)
    width = feat_store.shape[1]
    cap = serve_rows.shape[1]
    shape = jax.ShapeDtypeStruct
    halves = call_kernel(
        split_kernel, [shape((feat_store.shape[0], width // 2), F32)] * 2, [feat_store]
    )
    served = serve_rows.reshape(-1)
    parts = {}
    for j in order + [0]:
        (parts[j],) = call_kernel(
            partial_kernel,
            [shape((nodes, width), BF16 if j % 2 else F32)],
            [jnp.reshape(own ^ j, (1,)), served, wanted[j]] + list(halves),
            spaces="ss",
            scratch=[pltpu.VMEM((cap, width // 2), F32)] * 2,
        )
        if j:
            served, parts[j] = lax.optimization_barrier((served, parts[j]))
    halves = (slice(nodes // 2, nodes), slice(0, nodes // 2))
    for_own = []
    bit = 1
    while bit < blk_size:
        for j in [j for j in order if j & bit and j in parts]:
            part = parts.pop(j)
            if j == bit and 2 * bit >= blk_size:
                for_own.append([exchange(part[h].astype(BF16), sizes, 0, bit) for h in halves])
                continue
            arrived = exchange(part.astype(BF16), sizes, 0, bit)
            if j == bit:
                for_own.append([arrived[h] for h in halves])
            else:
                parts[j ^ bit] = parts[j ^ bit] + arrived.astype(F32)
        bit *= 2
    return (
        [parts[0][h] for h in halves],
        [[arrived[n] for arrived in for_own] for n in range(2)],
        [live_count[h] for h in halves],
    )


def mean_of(own_part, arrived, live_count):
    total = own_part
    for part in arrived:
        total = total + part.astype(F32)
    return (total / live_count).astype(BF16)


def forward(own_part, pooled, w_nbr, w_out):
    pre_act = own_part + jnp.dot(pooled, w_nbr, preferred_element_type=F32)
    hidden = (pre_act * jax.nn.sigmoid(pre_act)).astype(BF16)
    projected = with_layout_constraint(
        jnp.dot(hidden, w_out, preferred_element_type=F32), Layout((0, 1))
    )
    inv_norm = lax.rsqrt(jnp.mean(projected * projected, 1, keepdims=True) + 1e-06)
    embedding = (projected * inv_norm).astype(BF16)
    return embedding, projected, pre_act, hidden


def spread(block, sizes):
    blk_size = sizes[1]
    known = {0: block}
    bit = blk_size // 2
    while bit:
        known.update({j ^ bit: exchange(v, sizes, 0, bit) for j, v in list(known.items())})
        bit //= 2
    return [known[j] for j in range(1, blk_size)]


def pair_weights(q, i, positive, scale, columns):
    scores = lax.dot_general(q, i, LAST_DIMS, preferred_element_type=F32)
    return jax.nn.sigmoid(scores * scale - positive + MARGIN) / columns


def positive_of(q, i, scale):
    return jnp.sum(q.astype(F32) * i.astype(F32), 1, keepdims=True) * scale


def through_norm(d_embed, proj):
    inv = lax.rsqrt(jnp.mean(proj * proj, 1, keepdims=True) + 1e-06)
    interior = jnp.mean(d_embed * proj, 1, keepdims=True)
    return (inv * d_embed - proj * inv**3 * interior).astype(BF16)


def through_gate(d_proj, pre, w_out):
    d_hidden = lax.dot_general(d_proj, w_out, LAST_DIMS, preferred_element_type=F32)
    sig = jax.nn.sigmoid(pre)
    return (d_hidden * sig * (1.0 + pre * (1.0 - sig))).astype(BF16)


def query_kernel(group_size, *refs):
    queries, items = refs[0], refs[1 : 1 + group_size]
    proj, pre, w_out, tile, row_total, d_proj, d_pre = refs[1 + group_size :]
    q, own_items = queries[...], items[0][...]
    pairs, width = q.shape
    scale = width ** (-0.5)
    positive = positive_of(q, own_items, scale)
    total = jnp.zeros((pairs, 1), F32)
    d_query = jnp.zeros((pairs, width), F32)
    for j in range(group_size):
        block = items[j][...]
        weights = pair_weights(q, block, positive, scale, group_size * pairs)
        total += jnp.sum(weights, 1, keepdims=True)
        rounded = weights.astype(BF16)
        if j == 0:
            tile[...] = rounded
        d_query += jnp.dot(rounded, block, preferred_element_type=F32)
    row_total[...] = total
    d_query = (d_query - total * own_items.astype(F32)) * scale
    d_p = through_norm(d_query, proj[...])
    d_proj[...] = d_p
    d_pre[...] = through_gate(d_p, pre[...], w_out[...])


def item_kernel(group_size, core_ref, *refs):
    queries, items = refs[:group_size], refs[group_size : 2 * group_size]
    tile, row_total, proj, pre, w_out, d_proj_q, d_pre_q = refs[2 * group_size :][:7]
    hidden_q, hidden_i, feat, pooled_q, pooled_i, keep, give = refs[2 * group_size + 7 :]
    own_items, q = items[0][...], queries[0][...]
    pairs, width = q.shape
    scale = width ** (-0.5)
    d_item = (
        lax.dot_general(tile[...], q, OVER_ROWS, preferred_element_type=F32)
        - row_total[...] * q.astype(F32)
    )
    for j in range(1, group_size):
        block = queries[j][...]
        positive = positive_of(block, items[j][...], scale)
        weights = pair_weights(block, own_items, positive, scale, group_size * pairs).astype(BF16)
        d_item += lax.dot_general(weights, block, OVER_ROWS, preferred_element_type=F32)
    d_proj_i = through_norm(d_item * scale, proj[...])
    d_proj = (d_proj_q[...], d_proj_i)
    d_pre = (d_pre_q[...], through_gate(d_proj_i, pre[...], w_out[...]))
    feats = (feat[:pairs], feat[pairs:])
    pooled = (pooled_q[...], pooled_i[...])
    hiddens = (hidden_q, hidden_i)

    def over_nodes(left, right):
        return sum(
            lax.dot_general(a, b, OVER_ROWS, preferred_element_type=F32)
            for a, b in zip(left, right)
        )

    core = core_ref[0]
    hid = pre.shape[1]
    cut = hid // 2
    fold = cut * width // hid
    for half, out in ((1 - core, give), (core, keep)):
        rows = [jnp.where(half == 0, a, b) for a, b in zip(feats, pooled)]
        out[:width] = over_nodes(rows, d_pre).astype(out.dtype)
        for k in range(hid // width):
            columns = pl.ds(pl.multiple_of(half * cut + k * fold, fold), fold)
            grad = over_nodes([h[:, columns] for h in hiddens], d_proj)
            out[width:, k * width : (k + 1) * width] = grad.astype(out.dtype)


def cut_kernel(place, keep, arrived, *refs):
    pieces = refs
    rows = pieces[0].shape[0]
    for j, piece in enumerate(pieces):
        at = pl.ds(pl.multiple_of((place[0] ^ j) * rows, rows), rows)
        piece[...] = (keep[at, :].astype(F32) + arrived[at, :].astype(F32)).astype(piece.dtype)


def finish_kernel(place, block, other, *refs):
    outs, held, done = refs[:3], refs[3:6], refs[6]
    hid, width = held[2].shape
    cut = held[0].shape[0]
    fold = block.shape[0] - cut
    own = place[0]
    copies = [pltpu.make_async_copy(held[n], outs[n], done.at[n]) for n in range(3)]

    def half(index, at):
        return jnp.where(own == index, block[at], other[at]).astype(F32)

    for index in range(2):
        held[index][...] = half(index, (slice(0, cut), slice(None)))
        copies[index].start()
    for index in range(2):
        for k in range(hid // width):
            at = (slice(cut, cut + fold), slice(k * width, (k + 1) * width))
            start = index * (hid // 2) + k * fold
            held[2][start : start + fold, :] = half(index, at)
    copies[2].start()
    for copy in copies:
        copy.wait()


def backward(query_side, item_side, feat, pooled_q, pooled_i, w_out, group, own, sizes):
    blk_size = sizes[1]
    queries, *saved_q, hidden_q = query_side
    items, *saved_i, hidden_i = item_side
    pairs, width = queries.shape
    nodes, hid = 2 * pairs, hidden_q.shape[1]
    all_items = [items] + spread(items, sizes)
    all_queries = [queries] + spread(queries, sizes)
    shape = jax.ShapeDtypeStruct
    scores = 2 * pairs * pairs * width
    tile, row_total, d_proj_q, d_pre_q = call_kernel(
        functools.partial(query_kernel, blk_size),
        [
            shape((pairs, pairs), BF16),
            shape((pairs, 1), F32),
            shape((pairs, width), BF16),
            shape((pairs, hid), BF16),
        ],
        [queries] + all_items + saved_q + [w_out],
        2 * scores * blk_size + 2 * pairs * width * hid,
    )
    rows = width + width // 2
    plane = sizes[0] // 2
    core = group % 2
    across = group // 2
    if plane & (plane - 1) or rows % (16 * plane) or rows % (8 * plane * blk_size):
        plane = 1
    keep, give = call_kernel(
        functools.partial(item_kernel, blk_size),
        [shape((rows, hid), F32), shape((rows, hid), BF16)],
        [jnp.reshape(core, (1,))]
        + all_queries
        + all_items
        + [tile, row_total]
        + saved_i
        + [w_out, d_proj_q, d_pre_q, hidden_q, hidden_i, feat, pooled_q, pooled_i],
        2 * scores * blk_size + 2 * pairs * width * hid + 6 * nodes * width * hid,
        spaces="s",
    )
    pieces = call_kernel(
        cut_kernel,
        [shape((rows // plane, hid), BF16 if j else F32) for j in range(plane)],
        [jnp.reshape(across % plane, (1,)), keep, exchange(give, sizes, 1, 0)],
        spaces="s",
    )
    return sum_staged(pieces, core, across, own, sizes)


def sum_staged(pieces, core, across, own, sizes):
    blk_size = sizes[1]
    plane = len(pieces)

    def over_core(v, j):
        return exchange(v, sizes, j, 0)

    def over_plane(v, j):
        return exchange(v, sizes, 2 * j, 0)

    def over_blk(v, j):
        return exchange(v, sizes, 0, j)

    total = pieces[0]
    if plane > 1:
        for j in range(1, plane):
            total = total + over_plane(pieces[j], j).astype(F32)
        total = reduce_blocks(total, own, blk_size, over_blk)
        block = total.astype(BF16)
        block = gather_blocks(block, own, blk_size, over_blk)
        block = gather_blocks(block, across, plane, over_plane)
    else:
        halves = jnp.stack([jnp.where(core == c, total, 0.0) for c in range(2)])
        halves = lax.psum(halves, AXES)
        block = jnp.where(core == 0, halves[0], halves[1]).astype(BF16)
    other = over_core(block, 1)
    rows, hid = block.shape
    width = rows * 2 // 3
    outs = [(width, hid), (width, hid), (hid, width)]
    return tuple(
        call_kernel(
            finish_kernel,
            [jax.ShapeDtypeStruct(o, F32) for o in outs],
            [jnp.reshape(core, (1,)), block, other],
            spaces="s",
            outs_in="aaa",
            scratch=[pltpu.VMEM(o, F32) for o in outs] + [pltpu.SemaphoreType.DMA((3,))],
        )
    )


def on_device(sizes, self_feat, nbr_mask, neighbour_slot, serve_rows, feat_store, w_self, w_nbr, w_out):
    group = lax.axis_index("dp")
    own = lax.axis_index("blk")
    own_sums, arrived, live = pooled_sums(
        nbr_mask, neighbour_slot, serve_rows, feat_store, own, sizes
    )
    pairs = self_feat.shape[0] // 2
    own_part = lax.optimization_barrier(jnp.dot(self_feat, w_self, preferred_element_type=F32))
    pooled_i = mean_of(own_sums[0], arrived[0], live[0])
    items, *item_side = forward(own_part[pairs:], pooled_i, w_nbr, w_out)
    _, later = lax.optimization_barrier((items, arrived[1]))
    pooled_q = mean_of(own_sums[1], later, live[1])
    item_side = (items, *item_side)
    query_side = forward(own_part[:pairs], pooled_q, w_nbr, w_out)
    return backward(
        query_side, item_side, self_feat, pooled_q, pooled_i, w_out, group, own, sizes
    )


def solution(mesh):
    sizes = (mesh.shape["dp"], mesh.shape["blk"])
    in_specs = (
        P(("dp", "blk"), None),
        P(("dp", "blk"), None),
        P(("dp", "blk"), None),
        P(("dp", "blk"), None),
        P("blk", None),
        P(),
        P(),
        P(),
    )
    out_specs = (P(), P(), P())

    def body(*arrays):
        return on_device(sizes, *arrays)

    return jax.shard_map(
        body, mesh=mesh, in_specs=in_specs, out_specs=out_specs, check_vma=False
    )
```

```python
import functools

import jax
import jax.numpy as jnp
from jax import lax
from jax.experimental import pallas as pl
from jax.experimental.layout import Layout, with_layout_constraint
from jax.experimental.pallas import tpu as pltpu
from jax.sharding import PartitionSpec as P

MARGIN = 0.5
AXES = ("dp", "blk")
BF16 = jnp.bfloat16
F32 = jnp.float32
OVER_ROWS = (((0,), (0,)), ((), ()))
LAST_DIMS = (((1,), (1,)), ((), ()))


def exchange(value, sizes, flip_dp, flip_blk):
    dp_size, blk_size = sizes
    pairs = [
        (g * blk_size + b, (g ^ flip_dp) * blk_size + (b ^ flip_blk))
        for g in range(dp_size)
        for b in range(blk_size)
    ]
    return lax.ppermute(value, AXES, pairs)


def block_of(array, index, count):
    rows = array.shape[0] // count
    return lax.dynamic_slice_in_dim(array, index * rows, rows, 0)


def in_order(parts, own):
    ordered = []
    for place in range(len(parts)):
        block = parts[place]
        for own_value in range(1, len(parts)):
            block = jnp.where(own == own_value, parts[place ^ own_value], block)
        ordered.append(block)
    return jnp.concatenate(ordered, 0)


def reduce_blocks(array, own, count, send):
    arrived = [send(block_of(array, own ^ j, count).astype(BF16), j) for j in range(1, count)]
    total = block_of(array, own, count)
    for part in arrived:
        total = total + part.astype(F32)
    return total


def gather_blocks(block, own, count, send):
    return in_order([block] + [send(block, j) for j in range(1, count)], own)


def node_of_arrival(neighbour_slot, valid, count):
    slots = neighbour_slot.shape[1]
    low = 64
    node = lax.broadcasted_iota(jnp.int32, (1, slots), 1) // (slots // valid.shape[0])
    flat_valid = valid.reshape(1, slots)
    high_hot = lax.broadcasted_iota(jnp.int32, (slots // low, slots), 0) == neighbour_slot >> (low.bit_length() - 1)
    low_hot = lax.broadcasted_iota(jnp.int32, (low, slots), 0) == neighbour_slot & (low - 1)
    upper = ((node // 16 + 1) * flat_valid).astype(F32)
    lower = ((node % 16) * flat_valid).astype(F32)
    codes = jnp.concatenate(
        [jnp.where(low_hot, upper, 0.0), jnp.where(low_hot, lower, 0.0)], 0
    ).astype(BF16)
    found = lax.dot_general(
        high_hot.astype(BF16), codes, (((1,), (1,)), ((), ())), preferred_element_type=F32
    )
    found = found.astype(jnp.int32)
    return ((found[:, :low] - 1) * 16 + found[:, low:]).reshape(count, slots // count)


SPACES = {"s": pltpu.SMEM, "v": pltpu.VMEM, "a": pl.ANY}


def call_kernel(kernel, outs, args, flops=0, spaces="", outs_in="", scratch=()):
    moved = sum(a.size * a.dtype.itemsize for a in list(args) + list(outs)) if flops else 0
    return pl.pallas_call(
        kernel,
        out_shape=outs,
        in_specs=[pl.BlockSpec(memory_space=SPACES[c]) for c in spaces.ljust(len(args), "v")],
        out_specs=[pl.BlockSpec(memory_space=SPACES[c]) for c in outs_in.ljust(len(outs), "v")],
        scratch_shapes=list(scratch),
        compiler_params=pltpu.CompilerParams(vmem_limit_bytes=24 * 1024 * 1024),
        cost_estimate=pl.CostEstimate(flops=flops, bytes_accessed=moved, transcendentals=0),
    )(*args)


def split_kernel(store, left, right):
    rows, side = left.shape
    step = rows // 16

    def some_rows(i, carry):
        at = pl.ds(pl.multiple_of(i * step, step), step)
        block = store[at, :].astype(F32)
        left[at, :] = block[:, :side]
        right[at, :] = block[:, side:]
        return carry

    lax.fori_loop(0, 16, some_rows, 0)


def partial_kernel(requester, serve_rows, node_at, left, right, out, got_left, got_right):
    count = node_at.shape[1]
    first = requester[0] * count

    def some_rows(i, carry):
        base = i * 32
        wanted = [serve_rows[first + base + u] for u in range(32)]
        for tile in range(0, 32, 8):
            at = pl.ds(pl.multiple_of(base + tile, 8), 8)
            to_left, to_right = got_left.at[at, :], got_right.at[at, :]
            for u in range(8):
                row = pl.ds(wanted[tile + u], 1)
                to_left[u : u + 1, :] = left[row, :]
                to_right[u : u + 1, :] = right[row, :]
        return carry

    lax.fori_loop(0, count // 32, some_rows, 0)
    nodes = lax.broadcasted_iota(jnp.int32, (out.shape[0], count), 0)
    pick = (nodes == node_at[...]).astype(BF16)
    rows = jnp.concatenate([got_left[...], got_right[...]], 1).astype(BF16)
    out[...] = jnp.dot(pick, rows, preferred_element_type=F32).astype(out.dtype)


def pooled_sums(nbr_mask, neighbour_slot, serve_rows, feat_store, own, sizes):
    blk_size = sizes[1]
    nodes = nbr_mask.shape[0]
    first_col = lax.broadcasted_iota(jnp.int32, nbr_mask.shape, 1) == 0
    valid = jnp.where(first_col, 1, nbr_mask)
    live_count = jnp.sum(valid.astype(F32), 1, keepdims=True)
    node_at = node_of_arrival(neighbour_slot, valid, blk_size)
    order = list(range(blk_size - 1, 0, -1))
    wanted = {
        j: exchange(block_of(node_at, own ^ j, blk_size), sizes, 0, j) for j in order
    }
    wanted = dict(zip(wanted, lax.optimization_barrier(tuple(wanted.values()))))
    wanted[0] = block_of(node_at, own, blk_size)
    width = feat_store.shape[1]
    cap = serve_rows.shape[1]
    shape = jax.ShapeDtypeStruct
    halves = call_kernel(
        split_kernel, [shape((feat_store.shape[0], width // 2), F32)] * 2, [feat_store]
    )
    served = serve_rows.reshape(-1)
    parts = {}
    for j in order + [0]:
        (parts[j],) = call_kernel(
            partial_kernel,
            [shape((nodes, width), BF16 if j % 2 else F32)],
            [jnp.reshape(own ^ j, (1,)), served, wanted[j]] + list(halves),
            spaces="ss",
            scratch=[pltpu.VMEM((cap, width // 2), F32)] * 2,
        )
        if j:
            served, parts[j] = lax.optimization_barrier((served, parts[j]))
    halves = (slice(nodes // 2, nodes), slice(0, nodes // 2))
    for_own = []
    bit = 1
    while bit < blk_size:
        for j in [j for j in order if j & bit and j in parts]:
            part = parts.pop(j)
            if j == bit and 2 * bit >= blk_size:
                for_own.append([exchange(part[h].astype(BF16), sizes, 0, bit) for h in halves])
                continue
            arrived = exchange(part.astype(BF16), sizes, 0, bit)
            if j == bit:
                for_own.append([arrived[h] for h in halves])
            else:
                parts[j ^ bit] = parts[j ^ bit] + arrived.astype(F32)
        bit *= 2
    return (
        [parts[0][h] for h in halves],
        [[arrived[n] for arrived in for_own] for n in range(2)],
        [live_count[h] for h in halves],
    )


def mean_of(own_part, arrived, live_count):
    total = own_part
    for part in arrived:
        total = total + part.astype(F32)
    return (total / live_count).astype(BF16)


def forward(own_part, pooled, w_nbr, w_out):
    pre_act = own_part + jnp.dot(pooled, w_nbr, preferred_element_type=F32)
    hidden = (pre_act * jax.nn.sigmoid(pre_act)).astype(BF16)
    projected = with_layout_constraint(
        jnp.dot(hidden, w_out, preferred_element_type=F32), Layout((0, 1))
    )
    inv_norm = lax.rsqrt(jnp.mean(projected * projected, 1, keepdims=True) + 1e-06)
    embedding = (projected * inv_norm).astype(BF16)
    return embedding, projected, pre_act, hidden


def spread(block, sizes):
    blk_size = sizes[1]
    known = {0: block}
    bit = blk_size // 2
    while bit:
        known.update({j ^ bit: exchange(v, sizes, 0, bit) for j, v in list(known.items())})
        bit //= 2
    return [known[j] for j in range(1, blk_size)]


def pair_weights(q, i, positive, scale, columns):
    scores = lax.dot_general(q, i, LAST_DIMS, preferred_element_type=F32)
    return jax.nn.sigmoid(scores * scale - positive + MARGIN) / columns


def positive_of(q, i, scale):
    return jnp.sum(q.astype(F32) * i.astype(F32), 1, keepdims=True) * scale


def through_norm(d_embed, proj):
    inv = lax.rsqrt(jnp.mean(proj * proj, 1, keepdims=True) + 1e-06)
    interior = jnp.mean(d_embed * proj, 1, keepdims=True)
    return (inv * d_embed - proj * inv**3 * interior).astype(BF16)


def through_gate(d_proj, pre, w_out):
    d_hidden = lax.dot_general(d_proj, w_out, LAST_DIMS, preferred_element_type=F32)
    sig = jax.nn.sigmoid(pre)
    return (d_hidden * sig * (1.0 + pre * (1.0 - sig))).astype(BF16)


def query_kernel(group_size, *refs):
    queries, items = refs[0], refs[1 : 1 + group_size]
    proj, pre, w_out, tile, row_total, d_proj, d_pre = refs[1 + group_size :]
    q, own_items = queries[...], items[0][...]
    pairs, width = q.shape
    scale = width ** (-0.5)
    positive = positive_of(q, own_items, scale)
    total = jnp.zeros((pairs, 1), F32)
    d_query = jnp.zeros((pairs, width), F32)
    for j in range(group_size):
        block = items[j][...]
        weights = pair_weights(q, block, positive, scale, group_size * pairs)
        total += jnp.sum(weights, 1, keepdims=True)
        rounded = weights.astype(BF16)
        if j == 0:
            tile[...] = rounded
        d_query += jnp.dot(rounded, block, preferred_element_type=F32)
    row_total[...] = total
    d_query = (d_query - total * own_items.astype(F32)) * scale
    d_p = through_norm(d_query, proj[...])
    d_proj[...] = d_p
    d_pre[...] = through_gate(d_p, pre[...], w_out[...])


def item_kernel(group_size, core_ref, *refs):
    queries, items = refs[:group_size], refs[group_size : 2 * group_size]
    tile, row_total, proj, pre, w_out, d_proj_q, d_pre_q = refs[2 * group_size :][:7]
    hidden_q, hidden_i, feat, pooled_q, pooled_i, keep, give = refs[2 * group_size + 7 :]
    own_items, q = items[0][...], queries[0][...]
    pairs, width = q.shape
    scale = width ** (-0.5)
    d_item = (
        lax.dot_general(tile[...], q, OVER_ROWS, preferred_element_type=F32)
        - row_total[...] * q.astype(F32)
    )
    for j in range(1, group_size):
        block = queries[j][...]
        positive = positive_of(block, items[j][...], scale)
        weights = pair_weights(block, own_items, positive, scale, group_size * pairs).astype(BF16)
        d_item += lax.dot_general(weights, block, OVER_ROWS, preferred_element_type=F32)
    d_proj_i = through_norm(d_item * scale, proj[...])
    d_proj = (d_proj_q[...], d_proj_i)
    d_pre = (d_pre_q[...], through_gate(d_proj_i, pre[...], w_out[...]))
    feats = (feat[:pairs], feat[pairs:])
    pooled = (pooled_q[...], pooled_i[...])
    hiddens = (hidden_q, hidden_i)

    def over_nodes(left, right):
        return sum(
            lax.dot_general(a, b, OVER_ROWS, preferred_element_type=F32)
            for a, b in zip(left, right)
        )

    core = core_ref[0]
    hid = pre.shape[1]
    cut = hid // 2
    fold = cut * width // hid
    for half, out in ((1 - core, give), (core, keep)):
        rows = [jnp.where(half == 0, a, b) for a, b in zip(feats, pooled)]
        out[:width] = over_nodes(rows, d_pre).astype(out.dtype)
        for k in range(hid // width):
            columns = pl.ds(pl.multiple_of(half * cut + k * fold, fold), fold)
            grad = over_nodes([h[:, columns] for h in hiddens], d_proj)
            out[width:, k * width : (k + 1) * width] = grad.astype(out.dtype)


def cut_kernel(place, keep, arrived, *refs):
    pieces = refs
    rows = pieces[0].shape[0]
    for j, piece in enumerate(pieces):
        at = pl.ds(pl.multiple_of((place[0] ^ j) * rows, rows), rows)
        piece[...] = (keep[at, :].astype(F32) + arrived[at, :].astype(F32)).astype(piece.dtype)


def finish_kernel(place, block, other, *refs):
    outs, held, done = refs[:3], refs[3:6], refs[6]
    hid, width = held[2].shape
    cut = held[0].shape[0]
    fold = block.shape[0] - cut
    own = place[0]
    copies = [pltpu.make_async_copy(held[n], outs[n], done.at[n]) for n in range(3)]

    def half(index, at):
        return jnp.where(own == index, block[at], other[at]).astype(F32)

    for index in range(2):
        held[index][...] = half(index, (slice(0, cut), slice(None)))
        copies[index].start()
    for index in range(2):
        for k in range(hid // width):
            at = (slice(cut, cut + fold), slice(k * width, (k + 1) * width))
            start = index * (hid // 2) + k * fold
            held[2][start : start + fold, :] = half(index, at)
    copies[2].start()
    for copy in copies:
        copy.wait()


def backward(query_side, item_side, feat, pooled_q, pooled_i, w_out, group, own, sizes):
    blk_size = sizes[1]
    queries, *saved_q, hidden_q = query_side
    items, *saved_i, hidden_i = item_side
    pairs, width = queries.shape
    nodes, hid = 2 * pairs, hidden_q.shape[1]
    all_items = [items] + spread(items, sizes)
    all_queries = [queries] + spread(queries, sizes)
    shape = jax.ShapeDtypeStruct
    scores = 2 * pairs * pairs * width
    tile, row_total, d_proj_q, d_pre_q = call_kernel(
        functools.partial(query_kernel, blk_size),
        [
            shape((pairs, pairs), BF16),
            shape((pairs, 1), F32),
            shape((pairs, width), BF16),
            shape((pairs, hid), BF16),
        ],
        [queries] + all_items + saved_q + [w_out],
        2 * scores * blk_size + 2 * pairs * width * hid,
    )
    rows = width + width // 2
    plane = sizes[0] // 2
    core = group % 2
    across = group // 2
    if plane & (plane - 1) or rows % (16 * plane) or rows % (8 * plane * blk_size):
        plane = 1
    keep, give = call_kernel(
        functools.partial(item_kernel, blk_size),
        [shape((rows, hid), BF16), shape((rows, hid), BF16)],
        [jnp.reshape(core, (1,))]
        + all_queries
        + all_items
        + [tile, row_total]
        + saved_i
        + [w_out, d_proj_q, d_pre_q, hidden_q, hidden_i, feat, pooled_q, pooled_i],
        2 * scores * blk_size + 2 * pairs * width * hid + 6 * nodes * width * hid,
        spaces="s",
    )
    pieces = call_kernel(
        cut_kernel,
        [shape((rows // plane, hid), BF16 if j else F32) for j in range(plane)],
        [jnp.reshape(across % plane, (1,)), keep, exchange(give, sizes, 1, 0)],
        spaces="s",
    )
    return sum_staged(pieces, core, across, own, sizes)


def sum_staged(pieces, core, across, own, sizes):
    blk_size = sizes[1]
    plane = len(pieces)

    def over_core(v, j):
        return exchange(v, sizes, j, 0)

    def over_plane(v, j):
        return exchange(v, sizes, 2 * j, 0)

    def over_blk(v, j):
        return exchange(v, sizes, 0, j)

    total = pieces[0]
    if plane > 1:
        for j in range(1, plane):
            total = total + over_plane(pieces[j], j).astype(F32)
        total = reduce_blocks(total, own, blk_size, over_blk)
        block = total.astype(BF16)
        block = gather_blocks(block, own, blk_size, over_blk)
        block = gather_blocks(block, across, plane, over_plane)
    else:
        halves = jnp.stack([jnp.where(core == c, total, 0.0) for c in range(2)])
        halves = lax.psum(halves, AXES)
        block = jnp.where(core == 0, halves[0], halves[1]).astype(BF16)
    other = over_core(block, 1)
    rows, hid = block.shape
    width = rows * 2 // 3
    outs = [(width, hid), (width, hid), (hid, width)]
    return tuple(
        call_kernel(
            finish_kernel,
            [jax.ShapeDtypeStruct(o, F32) for o in outs],
            [jnp.reshape(core, (1,)), block, other],
            spaces="s",
            outs_in="aaa",
            scratch=[pltpu.VMEM(o, F32) for o in outs] + [pltpu.SemaphoreType.DMA((3,))],
        )
    )


def on_device(sizes, self_feat, nbr_mask, neighbour_slot, serve_rows, feat_store, w_self, w_nbr, w_out):
    group = lax.axis_index("dp")
    own = lax.axis_index("blk")
    own_sums, arrived, live = pooled_sums(
        nbr_mask, neighbour_slot, serve_rows, feat_store, own, sizes
    )
    pairs = self_feat.shape[0] // 2
    own_part = lax.optimization_barrier(jnp.dot(self_feat, w_self, preferred_element_type=F32))
    pooled_i = mean_of(own_sums[0], arrived[0], live[0])
    items, *item_side = forward(own_part[pairs:], pooled_i, w_nbr, w_out)
    _, later = lax.optimization_barrier((items, arrived[1]))
    pooled_q = mean_of(own_sums[1], later, live[1])
    item_side = (items, *item_side)
    query_side = forward(own_part[:pairs], pooled_q, w_nbr, w_out)
    return backward(
        query_side, item_side, self_feat, pooled_q, pooled_i, w_out, group, own, sizes
    )


def solution(mesh):
    sizes = (mesh.shape["dp"], mesh.shape["blk"])
    in_specs = (
        P(("dp", "blk"), None),
        P(("dp", "blk"), None),
        P(("dp", "blk"), None),
        P(("dp", "blk"), None),
        P("blk", None),
        P(),
        P(),
        P(),
    )
    out_specs = (P(), P(), P())

    def body(*arrays):
        return on_device(sizes, *arrays)

    return jax.shard_map(
        body, mesh=mesh, in_specs=in_specs, out_specs=out_specs, check_vma=False
    )
```

```python
import functools

import jax
import jax.numpy as jnp
from jax import lax
from jax.experimental import pallas as pl
from jax.experimental.layout import Layout, with_layout_constraint
from jax.experimental.pallas import tpu as pltpu
from jax.sharding import PartitionSpec as P

MARGIN = 0.5
AXES = ("dp", "blk")
BF16 = jnp.bfloat16
F32 = jnp.float32
OVER_ROWS = (((0,), (0,)), ((), ()))
LAST_DIMS = (((1,), (1,)), ((), ()))


def exchange(value, sizes, flip_dp, flip_blk):
    dp_size, blk_size = sizes
    pairs = [
        (g * blk_size + b, (g ^ flip_dp) * blk_size + (b ^ flip_blk))
        for g in range(dp_size)
        for b in range(blk_size)
    ]
    return lax.ppermute(value, AXES, pairs)


def block_of(array, index, count):
    rows = array.shape[0] // count
    return lax.dynamic_slice_in_dim(array, index * rows, rows, 0)


def in_order(parts, own):
    ordered = []
    for place in range(len(parts)):
        block = parts[place]
        for own_value in range(1, len(parts)):
            block = jnp.where(own == own_value, parts[place ^ own_value], block)
        ordered.append(block)
    return jnp.concatenate(ordered, 0)


def reduce_blocks(array, own, count, send):
    arrived = [send(block_of(array, own ^ j, count).astype(BF16), j) for j in range(1, count)]
    total = block_of(array, own, count)
    for part in arrived:
        total = total + part.astype(F32)
    return total


def gather_blocks(block, own, count, send):
    return in_order([block] + [send(block, j) for j in range(1, count)], own)


def node_of_arrival(neighbour_slot, valid, count):
    slots = neighbour_slot.shape[1]
    low = 64
    node = lax.broadcasted_iota(jnp.int32, (1, slots), 1) // (slots // valid.shape[0])
    flat_valid = valid.reshape(1, slots)
    high_hot = lax.broadcasted_iota(jnp.int32, (slots // low, slots), 0) == neighbour_slot >> (low.bit_length() - 1)
    low_hot = lax.broadcasted_iota(jnp.int32, (low, slots), 0) == neighbour_slot & (low - 1)
    upper = ((node // 16 + 1) * flat_valid).astype(F32)
    lower = ((node % 16) * flat_valid).astype(F32)
    codes = jnp.concatenate(
        [jnp.where(low_hot, upper, 0.0), jnp.where(low_hot, lower, 0.0)], 0
    ).astype(BF16)
    found = lax.dot_general(
        high_hot.astype(BF16), codes, (((1,), (1,)), ((), ())), preferred_element_type=F32
    )
    found = found.astype(jnp.int32)
    return ((found[:, :low] - 1) * 16 + found[:, low:]).reshape(count, slots // count)


SPACES = {"s": pltpu.SMEM, "v": pltpu.VMEM, "a": pl.ANY}


def call_kernel(kernel, outs, args, flops=0, spaces="", outs_in="", scratch=()):
    moved = sum(a.size * a.dtype.itemsize for a in list(args) + list(outs)) if flops else 0
    return pl.pallas_call(
        kernel,
        out_shape=outs,
        in_specs=[pl.BlockSpec(memory_space=SPACES[c]) for c in spaces.ljust(len(args), "v")],
        out_specs=[pl.BlockSpec(memory_space=SPACES[c]) for c in outs_in.ljust(len(outs), "v")],
        scratch_shapes=list(scratch),
        compiler_params=pltpu.CompilerParams(vmem_limit_bytes=24 * 1024 * 1024),
        cost_estimate=pl.CostEstimate(flops=flops, bytes_accessed=moved, transcendentals=0),
    )(*args)


def split_kernel(store, left, right):
    side = left.shape[1]
    step = store.shape[0] // 16

    def some_rows(i, carry):
        at = pl.ds(pl.multiple_of(i * step, step), step)
        block = store[at, :].astype(F32)
        left[at, :] = block[:, :side]
        right[at, :] = block[:, side:]
        return carry

    lax.fori_loop(0, 16, some_rows, 0)


def partial_kernel(requester, serve_rows, node_at, left, right, out, got_left, got_right):
    count = node_at.shape[1]
    first = requester[0] * count

    def some_rows(i, carry):
        base = i * 32
        wanted = [serve_rows[first + base + u] for u in range(32)]
        for tile in range(0, 32, 8):
            at = pl.ds(pl.multiple_of(base + tile, 8), 8)
            to_left, to_right = got_left.at[at, :], got_right.at[at, :]
            for u in range(8):
                row = pl.ds(wanted[tile + u], 1)
                to_left[u : u + 1, :] = left[row, :]
                to_right[u : u + 1, :] = right[row, :]
        return carry

    lax.fori_loop(0, count // 32, some_rows, 0)
    nodes = lax.broadcasted_iota(jnp.int32, (out.shape[0], count), 0)
    pick = (nodes == node_at[...]).astype(BF16)
    rows = jnp.concatenate([got_left[:count], got_right[:count]], 1).astype(BF16)
    out[...] = jnp.dot(pick, rows, preferred_element_type=F32).astype(out.dtype)


def pooled_sums(nbr_mask, neighbour_slot, serve_rows, feat_store, own, sizes):
    blk_size = sizes[1]
    nodes = nbr_mask.shape[0]
    first_col = lax.broadcasted_iota(jnp.int32, nbr_mask.shape, 1) == 0
    valid = jnp.where(first_col, 1, nbr_mask)
    live_count = jnp.sum(valid.astype(F32), 1, keepdims=True)
    node_at = node_of_arrival(neighbour_slot, valid, blk_size)
    order = list(range(blk_size - 1, 0, -1))
    wanted = {
        j: exchange(block_of(node_at, own ^ j, blk_size), sizes, 0, j) for j in order
    }
    wanted = dict(zip(wanted, lax.optimization_barrier(tuple(wanted.values()))))
    wanted[0] = block_of(node_at, own, blk_size)
    width = feat_store.shape[1]
    cap = serve_rows.shape[1]
    shape = jax.ShapeDtypeStruct
    tile = 8
    halves = call_kernel(
        split_kernel, [shape((feat_store.shape[0] + tile, width // 2), F32)] * 2, [feat_store]
    )
    served = serve_rows.reshape(-1)
    parts = {}
    for j in order + [0]:
        (parts[j],) = call_kernel(
            partial_kernel,
            [shape((nodes, width), BF16 if j % 2 else F32)],
            [jnp.reshape(own ^ j, (1,)), served, wanted[j]] + list(halves),
            spaces="ss",
            scratch=[pltpu.VMEM((cap + tile, width // 2), F32)] * 2,
        )
        if j:
            served, parts[j] = lax.optimization_barrier((served, parts[j]))
    halves = (slice(nodes // 2, nodes), slice(0, nodes // 2))
    for_own = []
    bit = 1
    while bit < blk_size:
        for j in [j for j in order if j & bit and j in parts]:
            part = parts.pop(j)
            if j == bit and 2 * bit >= blk_size:
                for_own.append([exchange(part[h].astype(BF16), sizes, 0, bit) for h in halves])
                continue
            arrived = exchange(part.astype(BF16), sizes, 0, bit)
            if j == bit:
                for_own.append([arrived[h] for h in halves])
            else:
                parts[j ^ bit] = parts[j ^ bit] + arrived.astype(F32)
        bit *= 2
    return (
        [parts[0][h] for h in halves],
        [[arrived[n] for arrived in for_own] for n in range(2)],
        [live_count[h] for h in halves],
    )


def mean_of(own_part, arrived, live_count):
    total = own_part
    for part in arrived:
        total = total + part.astype(F32)
    return (total / live_count).astype(BF16)


def forward(own_part, pooled, w_nbr, w_out):
    pre_act = own_part + jnp.dot(pooled, w_nbr, preferred_element_type=F32)
    hidden = (pre_act * jax.nn.sigmoid(pre_act)).astype(BF16)
    projected = with_layout_constraint(
        jnp.dot(hidden, w_out, preferred_element_type=F32), Layout((0, 1))
    )
    inv_norm = lax.rsqrt(jnp.mean(projected * projected, 1, keepdims=True) + 1e-06)
    embedding = (projected * inv_norm).astype(BF16)
    return embedding, projected, pre_act, hidden


def spread(block, sizes):
    blk_size = sizes[1]
    known = {0: block}
    bit = blk_size // 2
    while bit:
        known.update({j ^ bit: exchange(v, sizes, 0, bit) for j, v in list(known.items())})
        bit //= 2
    return [known[j] for j in range(1, blk_size)]


def pair_weights(q, i, positive, scale, columns):
    scores = lax.dot_general(q, i, LAST_DIMS, preferred_element_type=F32)
    return jax.nn.sigmoid(scores * scale - positive + MARGIN) / columns


def positive_of(q, i, scale):
    return jnp.sum(q.astype(F32) * i.astype(F32), 1, keepdims=True) * scale


def through_norm(d_embed, proj):
    inv = lax.rsqrt(jnp.mean(proj * proj, 1, keepdims=True) + 1e-06)
    interior = jnp.mean(d_embed * proj, 1, keepdims=True)
    return (inv * d_embed - proj * inv**3 * interior).astype(BF16)


def through_gate(d_proj, pre, w_out):
    d_hidden = lax.dot_general(d_proj, w_out, LAST_DIMS, preferred_element_type=F32)
    sig = jax.nn.sigmoid(pre)
    return (d_hidden * sig * (1.0 + pre * (1.0 - sig))).astype(BF16)


def query_kernel(group_size, *refs):
    queries, items = refs[0], refs[1 : 1 + group_size]
    proj, pre, w_out, tile, row_total, d_proj, d_pre = refs[1 + group_size :]
    q, own_items = queries[...], items[0][...]
    pairs, width = q.shape
    scale = width ** (-0.5)
    positive = positive_of(q, own_items, scale)
    total = jnp.zeros((pairs, 1), F32)
    d_query = jnp.zeros((pairs, width), F32)
    for j in range(group_size):
        block = items[j][...]
        weights = pair_weights(q, block, positive, scale, group_size * pairs)
        total += jnp.sum(weights, 1, keepdims=True)
        rounded = weights.astype(BF16)
        if j == 0:
            tile[...] = rounded
        d_query += jnp.dot(rounded, block, preferred_element_type=F32)
    row_total[...] = total
    d_query = (d_query - total * own_items.astype(F32)) * scale
    d_p = through_norm(d_query, proj[...])
    d_proj[...] = d_p
    d_pre[...] = through_gate(d_p, pre[...], w_out[...])


def item_kernel(group_size, core_ref, *refs):
    queries, items = refs[:group_size], refs[group_size : 2 * group_size]
    tile, row_total, proj, pre, w_out, d_proj_q, d_pre_q = refs[2 * group_size :][:7]
    hidden_q, hidden_i, feat, pooled_q, pooled_i, keep, give = refs[2 * group_size + 7 :]
    own_items, q = items[0][...], queries[0][...]
    pairs, width = q.shape
    scale = width ** (-0.5)
    d_item = (
        lax.dot_general(tile[...], q, OVER_ROWS, preferred_element_type=F32)
        - row_total[...] * q.astype(F32)
    )
    for j in range(1, group_size):
        block = queries[j][...]
        positive = positive_of(block, items[j][...], scale)
        weights = pair_weights(block, own_items, positive, scale, group_size * pairs).astype(BF16)
        d_item += lax.dot_general(weights, block, OVER_ROWS, preferred_element_type=F32)
    d_proj_i = through_norm(d_item * scale, proj[...])
    d_proj = (d_proj_q[...], d_proj_i)
    d_pre = (d_pre_q[...], through_gate(d_proj_i, pre[...], w_out[...]))
    feats = (feat[:pairs], feat[pairs:])
    pooled = (pooled_q[...], pooled_i[...])
    hiddens = (hidden_q, hidden_i)

    def over_nodes(left, right):
        return sum(
            lax.dot_general(a, b, OVER_ROWS, preferred_element_type=F32)
            for a, b in zip(left, right)
        )

    core = core_ref[0]
    hid = pre.shape[1]
    cut = hid // 2
    fold = cut * width // hid
    for half, out in ((1 - core, give), (core, keep)):
        rows = [jnp.where(half == 0, a, b) for a, b in zip(feats, pooled)]
        out[:width] = over_nodes(rows, d_pre).astype(out.dtype)
        for k in range(hid // width):
            columns = pl.ds(pl.multiple_of(half * cut + k * fold, fold), fold)
            grad = over_nodes([h[:, columns] for h in hiddens], d_proj)
            out[width:, k * width : (k + 1) * width] = grad.astype(out.dtype)


def cut_kernel(place, keep, arrived, *refs):
    pieces = refs
    rows = pieces[0].shape[0]
    for j, piece in enumerate(pieces):
        at = pl.ds(pl.multiple_of((place[0] ^ j) * rows, rows), rows)
        piece[...] = (keep[at, :].astype(F32) + arrived[at, :].astype(F32)).astype(piece.dtype)


def finish_kernel(place, block, other, *refs):
    outs, held, done = refs[:3], refs[3:6], refs[6]
    hid, width = held[2].shape
    cut = held[0].shape[0]
    fold = block.shape[0] - cut
    own = place[0]
    copies = [pltpu.make_async_copy(held[n], outs[n], done.at[n]) for n in range(3)]

    def half(index, at):
        return jnp.where(own == index, block[at], other[at]).astype(F32)

    for index in range(2):
        held[index][...] = half(index, (slice(0, cut), slice(None)))
        copies[index].start()
    for index in range(2):
        for k in range(hid // width):
            at = (slice(cut, cut + fold), slice(k * width, (k + 1) * width))
            start = index * (hid // 2) + k * fold
            held[2][start : start + fold, :] = half(index, at)
    copies[2].start()
    for copy in copies:
        copy.wait()


def backward(query_side, item_side, feat, pooled_q, pooled_i, w_out, group, own, sizes):
    blk_size = sizes[1]
    queries, *saved_q, hidden_q = query_side
    items, *saved_i, hidden_i = item_side
    pairs, width = queries.shape
    nodes, hid = 2 * pairs, hidden_q.shape[1]
    all_items = [items] + spread(items, sizes)
    all_queries = [queries] + spread(queries, sizes)
    shape = jax.ShapeDtypeStruct
    scores = 2 * pairs * pairs * width
    tile, row_total, d_proj_q, d_pre_q = call_kernel(
        functools.partial(query_kernel, blk_size),
        [
            shape((pairs, pairs), BF16),
            shape((pairs, 1), F32),
            shape((pairs, width), BF16),
            shape((pairs, hid), BF16),
        ],
        [queries] + all_items + saved_q + [w_out],
        2 * scores * blk_size + 2 * pairs * width * hid,
    )
    rows = width + width // 2
    plane = sizes[0] // 2
    core = group % 2
    across = group // 2
    if plane & (plane - 1) or rows % (16 * plane) or rows % (8 * plane * blk_size):
        plane = 1
    keep, give = call_kernel(
        functools.partial(item_kernel, blk_size),
        [shape((rows, hid), BF16), shape((rows, hid), BF16)],
        [jnp.reshape(core, (1,))]
        + all_queries
        + all_items
        + [tile, row_total]
        + saved_i
        + [w_out, d_proj_q, d_pre_q, hidden_q, hidden_i, feat, pooled_q, pooled_i],
        2 * scores * blk_size + 2 * pairs * width * hid + 6 * nodes * width * hid,
        spaces="s",
    )
    pieces = call_kernel(
        cut_kernel,
        [shape((rows // plane, hid), BF16 if j else F32) for j in range(plane)],
        [jnp.reshape(across % plane, (1,)), keep, exchange(give, sizes, 1, 0)],
        spaces="s",
    )
    return sum_staged(pieces, core, across, own, sizes)


def sum_staged(pieces, core, across, own, sizes):
    blk_size = sizes[1]
    plane = len(pieces)

    def over_core(v, j):
        return exchange(v, sizes, j, 0)

    def over_plane(v, j):
        return exchange(v, sizes, 2 * j, 0)

    def over_blk(v, j):
        return exchange(v, sizes, 0, j)

    total = pieces[0]
    if plane > 1:
        for j in range(1, plane):
            total = total + over_plane(pieces[j], j).astype(F32)
        total = reduce_blocks(total, own, blk_size, over_blk)
        block = total.astype(BF16)
        block = gather_blocks(block, own, blk_size, over_blk)
        block = gather_blocks(block, across, plane, over_plane)
    else:
        halves = jnp.stack([jnp.where(core == c, total, 0.0) for c in range(2)])
        halves = lax.psum(halves, AXES)
        block = jnp.where(core == 0, halves[0], halves[1]).astype(BF16)
    other = over_core(block, 1)
    rows, hid = block.shape
    width = rows * 2 // 3
    outs = [(width, hid), (width, hid), (hid, width)]
    return tuple(
        call_kernel(
            finish_kernel,
            [jax.ShapeDtypeStruct(o, F32) for o in outs],
            [jnp.reshape(core, (1,)), block, other],
            spaces="s",
            outs_in="aaa",
            scratch=[pltpu.VMEM(o, F32) for o in outs] + [pltpu.SemaphoreType.DMA((3,))],
        )
    )


def on_device(sizes, self_feat, nbr_mask, neighbour_slot, serve_rows, feat_store, w_self, w_nbr, w_out):
    group = lax.axis_index("dp")
    own = lax.axis_index("blk")
    own_sums, arrived, live = pooled_sums(
        nbr_mask, neighbour_slot, serve_rows, feat_store, own, sizes
    )
    pairs = self_feat.shape[0] // 2
    own_part = lax.optimization_barrier(jnp.dot(self_feat, w_self, preferred_element_type=F32))
    pooled_i = mean_of(own_sums[0], arrived[0], live[0])
    items, *item_side = forward(own_part[pairs:], pooled_i, w_nbr, w_out)
    _, later = lax.optimization_barrier((items, arrived[1]))
    pooled_q = mean_of(own_sums[1], later, live[1])
    item_side = (items, *item_side)
    query_side = forward(own_part[:pairs], pooled_q, w_nbr, w_out)
    return backward(
        query_side, item_side, self_feat, pooled_q, pooled_i, w_out, group, own, sizes
    )


def solution(mesh):
    sizes = (mesh.shape["dp"], mesh.shape["blk"])
    in_specs = (
        P(("dp", "blk"), None),
        P(("dp", "blk"), None),
        P(("dp", "blk"), None),
        P(("dp", "blk"), None),
        P("blk", None),
        P(),
        P(),
        P(),
    )
    out_specs = (P(), P(), P())

    def body(*arrays):
        return on_device(sizes, *arrays)

    return jax.shard_map(
        body, mesh=mesh, in_specs=in_specs, out_specs=out_specs, check_vma=False
    )
```

```python
import functools

import jax
import jax.numpy as jnp
from jax import lax
from jax.experimental import pallas as pl
from jax.experimental.layout import Layout, with_layout_constraint
from jax.experimental.pallas import tpu as pltpu
from jax.sharding import PartitionSpec as P

MARGIN = 0.5
AXES = ("dp", "blk")
BF16 = jnp.bfloat16
F32 = jnp.float32
OVER_ROWS = (((0,), (0,)), ((), ()))
LAST_DIMS = (((1,), (1,)), ((), ()))


def exchange(value, sizes, flip_dp, flip_blk):
    dp_size, blk_size = sizes
    pairs = [
        (g * blk_size + b, (g ^ flip_dp) * blk_size + (b ^ flip_blk))
        for g in range(dp_size)
        for b in range(blk_size)
    ]
    return lax.ppermute(value, AXES, pairs)


def block_of(array, index, count):
    rows = array.shape[0] // count
    return lax.dynamic_slice_in_dim(array, index * rows, rows, 0)


def in_order(parts, own):
    ordered = []
    for place in range(len(parts)):
        block = parts[place]
        for own_value in range(1, len(parts)):
            block = jnp.where(own == own_value, parts[place ^ own_value], block)
        ordered.append(block)
    return jnp.concatenate(ordered, 0)


def reduce_blocks(array, own, count, send):
    arrived = [send(block_of(array, own ^ j, count).astype(BF16), j) for j in range(1, count)]
    total = block_of(array, own, count)
    for part in arrived:
        total = total + part.astype(F32)
    return total


def gather_blocks(block, own, count, send):
    return in_order([block] + [send(block, j) for j in range(1, count)], own)


def node_of_arrival(neighbour_slot, valid, count):
    slots = neighbour_slot.shape[1]
    low = 64
    node = lax.broadcasted_iota(jnp.int32, (1, slots), 1) // (slots // valid.shape[0])
    flat_valid = valid.reshape(1, slots)
    high_hot = lax.broadcasted_iota(jnp.int32, (slots // low, slots), 0) == neighbour_slot >> (low.bit_length() - 1)
    low_hot = lax.broadcasted_iota(jnp.int32, (low, slots), 0) == neighbour_slot & (low - 1)
    upper = ((node // 16 + 1) * flat_valid).astype(F32)
    lower = ((node % 16) * flat_valid).astype(F32)
    codes = jnp.concatenate(
        [jnp.where(low_hot, upper, 0.0), jnp.where(low_hot, lower, 0.0)], 0
    ).astype(BF16)
    found = lax.dot_general(
        high_hot.astype(BF16), codes, (((1,), (1,)), ((), ())), preferred_element_type=F32
    )
    found = found.astype(jnp.int32)
    return ((found[:, :low] - 1) * 16 + found[:, low:]).reshape(count, slots // count)


SPACES = {"s": pltpu.SMEM, "v": pltpu.VMEM, "a": pl.ANY}


def call_kernel(kernel, outs, args, flops=0, spaces="", outs_in="", scratch=()):
    moved = sum(a.size * a.dtype.itemsize for a in list(args) + list(outs)) if flops else 0
    return pl.pallas_call(
        kernel,
        out_shape=outs,
        in_specs=[pl.BlockSpec(memory_space=SPACES[c]) for c in spaces.ljust(len(args), "v")],
        out_specs=[pl.BlockSpec(memory_space=SPACES[c]) for c in outs_in.ljust(len(outs), "v")],
        scratch_shapes=list(scratch),
        compiler_params=pltpu.CompilerParams(vmem_limit_bytes=24 * 1024 * 1024),
        cost_estimate=pl.CostEstimate(flops=flops, bytes_accessed=moved, transcendentals=0),
    )(*args)


def split_kernel(store, left, right):
    side = left.shape[1]
    step = store.shape[0] // 16

    def some_rows(i, carry):
        at = pl.ds(pl.multiple_of(i * step, step), step)
        block = store[at, :].astype(F32)
        left[at, :] = block[:, :side]
        right[at, :] = block[:, side:]
        return carry

    lax.fori_loop(0, 16, some_rows, 0)


def partial_kernel(requester, serve_rows, node_at, left, right, out, got_left, got_right):
    count = node_at.shape[1]
    first = requester[0] * count

    def some_rows(i, carry):
        base = i * 64
        wanted = [serve_rows[first + base + u] for u in range(64)]
        for tile in range(0, 64, 8):
            at = pl.ds(pl.multiple_of(base + tile, 8), 8)
            to_left, to_right = got_left.at[at, :], got_right.at[at, :]
            for u in range(8):
                row = pl.ds(wanted[tile + u], 1)
                to_left[u : u + 1, :] = left[row, :]
                to_right[u : u + 1, :] = right[row, :]
        return carry

    lax.fori_loop(0, count // 64, some_rows, 0)
    nodes = lax.broadcasted_iota(jnp.int32, (out.shape[0], count), 0)
    pick = (nodes == node_at[...]).astype(BF16)
    rows = jnp.concatenate([got_left[:count], got_right[:count]], 1).astype(BF16)
    out[...] = jnp.dot(pick, rows, preferred_element_type=F32).astype(out.dtype)


def pooled_sums(nbr_mask, neighbour_slot, serve_rows, feat_store, own, sizes):
    blk_size = sizes[1]
    nodes = nbr_mask.shape[0]
    first_col = lax.broadcasted_iota(jnp.int32, nbr_mask.shape, 1) == 0
    valid = jnp.where(first_col, 1, nbr_mask)
    live_count = jnp.sum(valid.astype(F32), 1, keepdims=True)
    node_at = node_of_arrival(neighbour_slot, valid, blk_size)
    order = list(range(blk_size - 1, 0, -1))
    wanted = {
        j: exchange(block_of(node_at, own ^ j, blk_size), sizes, 0, j) for j in order
    }
    wanted = dict(zip(wanted, lax.optimization_barrier(tuple(wanted.values()))))
    wanted[0] = block_of(node_at, own, blk_size)
    width = feat_store.shape[1]
    cap = serve_rows.shape[1]
    shape = jax.ShapeDtypeStruct
    tile = 8
    halves = call_kernel(
        split_kernel, [shape((feat_store.shape[0] + tile, width // 2), F32)] * 2, [feat_store]
    )
    served = serve_rows.reshape(-1)
    parts = {}
    for j in order + [0]:
        (parts[j],) = call_kernel(
            partial_kernel,
            [shape((nodes, width), BF16 if j % 2 else F32)],
            [jnp.reshape(own ^ j, (1,)), served, wanted[j]] + list(halves),
            spaces="ss",
            scratch=[pltpu.VMEM((cap + tile, width // 2), F32)] * 2,
        )
        if j:
            served, parts[j] = lax.optimization_barrier((served, parts[j]))
    halves = (slice(nodes // 2, nodes), slice(0, nodes // 2))
    for_own = []
    bit = 1
    while bit < blk_size:
        for j in [j for j in order if j & bit and j in parts]:
            part = parts.pop(j)
            if j == bit and 2 * bit >= blk_size:
                for_own.append([exchange(part[h].astype(BF16), sizes, 0, bit) for h in halves])
                continue
            arrived = exchange(part.astype(BF16), sizes, 0, bit)
            if j == bit:
                for_own.append([arrived[h] for h in halves])
            else:
                parts[j ^ bit] = parts[j ^ bit] + arrived.astype(F32)
        bit *= 2
    return (
        [parts[0][h] for h in halves],
        [[arrived[n] for arrived in for_own] for n in range(2)],
        [live_count[h] for h in halves],
    )


def mean_of(own_part, arrived, live_count):
    total = own_part
    for part in arrived:
        total = total + part.astype(F32)
    return (total / live_count).astype(BF16)


def forward(own_part, pooled, w_nbr, w_out):
    pre_act = own_part + jnp.dot(pooled, w_nbr, preferred_element_type=F32)
    hidden = (pre_act * jax.nn.sigmoid(pre_act)).astype(BF16)
    projected = with_layout_constraint(
        jnp.dot(hidden, w_out, preferred_element_type=F32), Layout((0, 1))
    )
    inv_norm = lax.rsqrt(jnp.mean(projected * projected, 1, keepdims=True) + 1e-06)
    embedding = (projected * inv_norm).astype(BF16)
    return embedding, projected, pre_act, hidden


def spread(block, sizes):
    blk_size = sizes[1]
    known = {0: block}
    bit = blk_size // 2
    while bit:
        known.update({j ^ bit: exchange(v, sizes, 0, bit) for j, v in list(known.items())})
        bit //= 2
    return [known[j] for j in range(1, blk_size)]


def pair_weights(q, i, positive, scale, columns):
    scores = lax.dot_general(q, i, LAST_DIMS, preferred_element_type=F32)
    return jax.nn.sigmoid(scores * scale - positive + MARGIN) / columns


def positive_of(q, i, scale):
    return jnp.sum(q.astype(F32) * i.astype(F32), 1, keepdims=True) * scale


def through_norm(d_embed, proj):
    inv = lax.rsqrt(jnp.mean(proj * proj, 1, keepdims=True) + 1e-06)
    interior = jnp.mean(d_embed * proj, 1, keepdims=True)
    return (inv * d_embed - proj * inv**3 * interior).astype(BF16)


def through_gate(d_proj, pre, w_out):
    d_hidden = lax.dot_general(d_proj, w_out, LAST_DIMS, preferred_element_type=F32)
    sig = jax.nn.sigmoid(pre)
    return (d_hidden * sig * (1.0 + pre * (1.0 - sig))).astype(BF16)


def query_kernel(group_size, *refs):
    queries, items = refs[0], refs[1 : 1 + group_size]
    proj, pre, w_out, tile, row_total, d_proj, d_pre = refs[1 + group_size :]
    q, own_items = queries[...], items[0][...]
    pairs, width = q.shape
    scale = width ** (-0.5)
    positive = positive_of(q, own_items, scale)
    total = jnp.zeros((pairs, 1), F32)
    d_query = jnp.zeros((pairs, width), F32)
    for j in range(group_size):
        block = items[j][...]
        weights = pair_weights(q, block, positive, scale, group_size * pairs)
        total += jnp.sum(weights, 1, keepdims=True)
        rounded = weights.astype(BF16)
        if j == 0:
            tile[...] = rounded
        d_query += jnp.dot(rounded, block, preferred_element_type=F32)
    row_total[...] = total
    d_query = (d_query - total * own_items.astype(F32)) * scale
    d_p = through_norm(d_query, proj[...])
    d_proj[...] = d_p
    d_pre[...] = through_gate(d_p, pre[...], w_out[...])


def item_kernel(group_size, core_ref, *refs):
    queries, items = refs[:group_size], refs[group_size : 2 * group_size]
    tile, row_total, proj, pre, w_out, d_proj_q, d_pre_q = refs[2 * group_size :][:7]
    hidden_q, hidden_i, feat, pooled_q, pooled_i, keep, give = refs[2 * group_size + 7 :]
    own_items, q = items[0][...], queries[0][...]
    pairs, width = q.shape
    scale = width ** (-0.5)
    d_item = (
        lax.dot_general(tile[...], q, OVER_ROWS, preferred_element_type=F32)
        - row_total[...] * q.astype(F32)
    )
    for j in range(1, group_size):
        block = queries[j][...]
        positive = positive_of(block, items[j][...], scale)
        weights = pair_weights(block, own_items, positive, scale, group_size * pairs).astype(BF16)
        d_item += lax.dot_general(weights, block, OVER_ROWS, preferred_element_type=F32)
    d_proj_i = through_norm(d_item * scale, proj[...])
    d_proj = (d_proj_q[...], d_proj_i)
    d_pre = (d_pre_q[...], through_gate(d_proj_i, pre[...], w_out[...]))
    feats = (feat[:pairs], feat[pairs:])
    pooled = (pooled_q[...], pooled_i[...])
    hiddens = (hidden_q, hidden_i)

    def over_nodes(left, right):
        return sum(
            lax.dot_general(a, b, OVER_ROWS, preferred_element_type=F32)
            for a, b in zip(left, right)
        )

    core = core_ref[0]
    hid = pre.shape[1]
    cut = hid // 2
    fold = cut * width // hid
    for half, out in ((1 - core, give), (core, keep)):
        rows = [jnp.where(half == 0, a, b) for a, b in zip(feats, pooled)]
        out[:width] = over_nodes(rows, d_pre).astype(out.dtype)
        for k in range(hid // width):
            columns = pl.ds(pl.multiple_of(half * cut + k * fold, fold), fold)
            grad = over_nodes([h[:, columns] for h in hiddens], d_proj)
            out[width:, k * width : (k + 1) * width] = grad.astype(out.dtype)


def cut_kernel(place, keep, arrived, *refs):
    pieces = refs
    rows = pieces[0].shape[0]
    for j, piece in enumerate(pieces):
        at = pl.ds(pl.multiple_of((place[0] ^ j) * rows, rows), rows)
        piece[...] = (keep[at, :].astype(F32) + arrived[at, :].astype(F32)).astype(piece.dtype)


def finish_kernel(place, block, other, *refs):
    outs, held, done = refs[:3], refs[3:6], refs[6]
    hid, width = held[2].shape
    cut = held[0].shape[0]
    fold = block.shape[0] - cut
    own = place[0]
    copies = [pltpu.make_async_copy(held[n], outs[n], done.at[n]) for n in range(3)]

    def half(index, at):
        return jnp.where(own == index, block[at], other[at]).astype(F32)

    for index in range(2):
        held[index][...] = half(index, (slice(0, cut), slice(None)))
        copies[index].start()
    for index in range(2):
        for k in range(hid // width):
            at = (slice(cut, cut + fold), slice(k * width, (k + 1) * width))
            start = index * (hid // 2) + k * fold
            held[2][start : start + fold, :] = half(index, at)
    copies[2].start()
    for copy in copies:
        copy.wait()


def backward(query_side, item_side, feat, pooled_q, pooled_i, w_out, group, own, sizes):
    blk_size = sizes[1]
    queries, *saved_q, hidden_q = query_side
    items, *saved_i, hidden_i = item_side
    pairs, width = queries.shape
    nodes, hid = 2 * pairs, hidden_q.shape[1]
    all_items = [items] + spread(items, sizes)
    all_queries = [queries] + spread(queries, sizes)
    shape = jax.ShapeDtypeStruct
    scores = 2 * pairs * pairs * width
    tile, row_total, d_proj_q, d_pre_q = call_kernel(
        functools.partial(query_kernel, blk_size),
        [
            shape((pairs, pairs), BF16),
            shape((pairs, 1), F32),
            shape((pairs, width), BF16),
            shape((pairs, hid), BF16),
        ],
        [queries] + all_items + saved_q + [w_out],
        2 * scores * blk_size + 2 * pairs * width * hid,
    )
    rows = width + width // 2
    plane = sizes[0] // 2
    core = group % 2
    across = group // 2
    if plane & (plane - 1) or rows % (16 * plane) or rows % (8 * plane * blk_size):
        plane = 1
    keep, give = call_kernel(
        functools.partial(item_kernel, blk_size),
        [shape((rows, hid), BF16), shape((rows, hid), BF16)],
        [jnp.reshape(core, (1,))]
        + all_queries
        + all_items
        + [tile, row_total]
        + saved_i
        + [w_out, d_proj_q, d_pre_q, hidden_q, hidden_i, feat, pooled_q, pooled_i],
        2 * scores * blk_size + 2 * pairs * width * hid + 6 * nodes * width * hid,
        spaces="s",
    )
    pieces = call_kernel(
        cut_kernel,
        [shape((rows // plane, hid), BF16 if j else F32) for j in range(plane)],
        [jnp.reshape(across % plane, (1,)), keep, exchange(give, sizes, 1, 0)],
        spaces="s",
    )
    return sum_staged(pieces, core, across, own, sizes)


def sum_staged(pieces, core, across, own, sizes):
    blk_size = sizes[1]
    plane = len(pieces)

    def over_core(v, j):
        return exchange(v, sizes, j, 0)

    def over_plane(v, j):
        return exchange(v, sizes, 2 * j, 0)

    def over_blk(v, j):
        return exchange(v, sizes, 0, j)

    total = pieces[0]
    if plane > 1:
        for j in range(1, plane):
            total = total + over_plane(pieces[j], j).astype(F32)
        total = reduce_blocks(total, own, blk_size, over_blk)
        block = total.astype(BF16)
        block = gather_blocks(block, own, blk_size, over_blk)
        block = gather_blocks(block, across, plane, over_plane)
    else:
        halves = jnp.stack([jnp.where(core == c, total, 0.0) for c in range(2)])
        halves = lax.psum(halves, AXES)
        block = jnp.where(core == 0, halves[0], halves[1]).astype(BF16)
    other = over_core(block, 1)
    rows, hid = block.shape
    width = rows * 2 // 3
    outs = [(width, hid), (width, hid), (hid, width)]
    return tuple(
        call_kernel(
            finish_kernel,
            [jax.ShapeDtypeStruct(o, F32) for o in outs],
            [jnp.reshape(core, (1,)), block, other],
            spaces="s",
            outs_in="aaa",
            scratch=[pltpu.VMEM(o, F32) for o in outs] + [pltpu.SemaphoreType.DMA((3,))],
        )
    )


def on_device(sizes, self_feat, nbr_mask, neighbour_slot, serve_rows, feat_store, w_self, w_nbr, w_out):
    group = lax.axis_index("dp")
    own = lax.axis_index("blk")
    own_sums, arrived, live = pooled_sums(
        nbr_mask, neighbour_slot, serve_rows, feat_store, own, sizes
    )
    pairs = self_feat.shape[0] // 2
    own_part = lax.optimization_barrier(jnp.dot(self_feat, w_self, preferred_element_type=F32))
    pooled_i = mean_of(own_sums[0], arrived[0], live[0])
    items, *item_side = forward(own_part[pairs:], pooled_i, w_nbr, w_out)
    _, later = lax.optimization_barrier((items, arrived[1]))
    pooled_q = mean_of(own_sums[1], later, live[1])
    item_side = (items, *item_side)
    query_side = forward(own_part[:pairs], pooled_q, w_nbr, w_out)
    return backward(
        query_side, item_side, self_feat, pooled_q, pooled_i, w_out, group, own, sizes
    )


def solution(mesh):
    sizes = (mesh.shape["dp"], mesh.shape["blk"])
    in_specs = (
        P(("dp", "blk"), None),
        P(("dp", "blk"), None),
        P(("dp", "blk"), None),
        P(("dp", "blk"), None),
        P("blk", None),
        P(),
        P(),
        P(),
    )
    out_specs = (P(), P(), P())

    def body(*arrays):
        return on_device(sizes, *arrays)

    return jax.shard_map(
        body, mesh=mesh, in_specs=in_specs, out_specs=out_specs, check_vma=False
    )
```
